512 devices in a mesh: expert: 64 (over y, z), tensor: 8 (over x, core).
Axes of the slice: x: 4, y: 8, z: 8, core: 2. Of those that a mesh axis runs over, the one named last changes fastest.
Arguments:
- grad_out: bfloat16 [4096, 6144], P('expert', 'tensor'), may hold values from -3 to 3
- routes: int32 [4096, 2], P('expert'), may hold values from 0 to 7, all different within a row; in each aligned block of 64 rows (0 to 63, 64 to 127, ...) at most 24 rows name the same one
- gates: bfloat16 [4096, 2], P('expert'), may hold values from 0.099609375 to 1
- w_down: bfloat16 [65536, 6144], P('expert', 'tensor'), may hold values from -0.0625 to 0.0625
- gate_pre: bfloat16 [1536, 65536], P(None, ('expert', 'tensor')), may hold values from -5 to 5
- up_pre: bfloat16 [1536, 65536], P(None, ('expert', 'tensor')), may hold values from -5 to 5
Outputs:
- w_down_grad: bfloat16 [65536, 6144], P('expert', 'tensor')
- gate_pre_grad: bfloat16 [1536, 65536], P(None, ('expert', 'tensor'))
- up_pre_grad: bfloat16 [1536, 65536], P(None, ('expert', 'tensor'))
- gate_grad: float32 [4096, 2], P('expert')
The draws below stay inside these ranges and needn't reach their ends.
Inputs may be any that keep to these rules, and one draw needn't show every extreme that they name: `routes`: among the 64 tokens of one index of expert, no expert is named more than 24 times, a bound that some block reaches. The two experts of a token differ.
All inputs are finite; a program needn't handle non-finite values.
Results may differ from the reference program's by a relative error of at most 0.019.
Values may be sent and summed in bfloat16 or wider, within the bound.
No kernel may reach another device: no remote copies, remote signals or barrier semaphores. Data moves between devices by JAX's collectives and lax.ppermute only.
A program may use at most 64 MiB of HBM per device.

```python
import math
import jax
import jax.numpy as jnp
import numpy as np
from jax import lax

D = 6144
FF = 8192
EXPERTS = 8
TOP = 2
TOK_DEV = 64
CAP = 24
SLOTS = 1536
TOKENS = 4096
N_EXPERT = 64
N_TENSOR = 8


def levels(own_key, dims, pieces, least, high):
    level, own = 1.0, jax.random.fold_in(own_key, 6)
    for position, shards_of in pieces:
        steps = jnp.exp(jax.random.uniform(jax.random.fold_in(own, position), (shards_of,), jnp.float32, least / len(pieces), high / len(pieces)))
        level = level * jnp.repeat(steps, dims[position] // shards_of).reshape([-1 if axis == position else 1 for axis in range(len(dims))])
    return level


def deal_out(key, own, number, rows, count, top, bound, skew):
    order = jax.random.permutation(key, count)
    heavy_load, ordinary = shares(count, rows * top, bound, skew, True), shares(count, rows * top, bound, skew, False)
    places = jnp.arange(count)

    def named(tallies, turn):
        used = int((tallies > 0).sum())
        fixed = max(1, used // 4)
        passed = fixed + (places - fixed + turn * (used - fixed)) % max(1, count - fixed)
        return jnp.zeros((count,), jnp.int32).at[order[jnp.where(places < fixed, places, passed)]].set(jnp.asarray(tallies, jnp.int32))

    tallies = jnp.where(number % 4 == 0, named(heavy_load, number // 4), named(ordinary, number - number // 4 - 1))
    mixed = jax.random.permutation(jax.random.fold_in(own, 3), count)
    source_of, taker = mixed[0:count // 2 * 2:2], mixed[1:count // 2 * 2:2]
    margin = jnp.minimum(tallies[source_of] - 1, bound - tallies[taker]) // 2
    margin = jnp.where((source_of == order[0]) | (taker == order[0]) | (tallies[taker] == 0), 0, jnp.maximum(margin, 0))
    passed = jax.random.randint(jax.random.fold_in(own, 4), (count // 2,), 0, 1 << 20) % (margin + 1)
    tallies = tallies.at[source_of].add(-passed).at[taker].add(passed)
    items = jnp.searchsorted(jnp.cumsum(tallies), jnp.arange(rows * top), side="right").astype(jnp.int32)
    table = items.reshape(top, rows).T
    table = table[jax.random.permutation(jax.random.fold_in(own, 1), rows)]
    turn = jax.random.randint(jax.random.fold_in(own, 2), (rows, 1), 0, top)
    return jnp.take_along_axis(table, (jnp.arange(top)[None, :] + turn) % top, axis=1)


def shares(number_of, total, limit, lean, full):
    loads = [(1 << 20) // math.isqrt(rank ** lean) + 1 for rank in range(1, number_of + 1)]
    largest = limit if full else min(limit, max(-(-total // number_of), total * loads[0] // sum(loads)))
    least = 1 if total - largest >= number_of - 1 else 0
    holding, rest = [largest] + [least] * (number_of - 1), total - largest - least * (number_of - 1)
    while rest > 0:
        candidates = [i for i in range(1, number_of) if holding[i] < largest] or [i for i in range(1, number_of) if holding[i] < limit]
        mass, budget = sum([loads[i] for i in candidates]), rest
        for i in candidates:
            more = min(limit - holding[i], max(1, budget * loads[i] // mass), rest)
            holding[i] = holding[i] + more
            rest = rest - more
    return np.array(holding)


def normal_values(stream_key, dims, spread, limit, shards=(), kind=jnp.bfloat16):
    drawn = spread * jax.random.normal(stream_key, dims, jnp.float32)
    if shards:
        drawn = drawn * levels(stream_key, dims, shards, -0.22, 0.18)
    return jnp.clip(drawn, -limit, limit).astype(kind)


def setup_inputs(seed: int = 0) -> dict:
    streams_of = jax.random.split(jax.random.key(seed), 7)
    grad_out = normal_values(streams_of[0], (TOKENS, D), 0.5, 3.0, ((0, 64), (1, 8)))
    routes_keys = jax.random.split(jax.random.fold_in(streams_of[1], 1), TOKENS // TOK_DEV)
    routes_turns = jax.random.permutation(jax.random.fold_in(streams_of[1], 3), TOKENS // TOK_DEV)
    routes = jax.vmap(lambda own, number: deal_out(jax.random.fold_in(streams_of[1], 2), own, number, TOK_DEV, EXPERTS, TOP, CAP, 2))(routes_keys, routes_turns).reshape((TOKENS, TOP))
    gates = jnp.clip(0.099609375 + 0.9003906 * jax.random.uniform(streams_of[2], (TOKENS, TOP), jnp.float32) ** levels(streams_of[2], (TOKENS, TOP), ((0, 64),), -0.2, 0.2), 0.099609375, 1.0).astype(jnp.bfloat16)
    w_down = normal_values(streams_of[3], (EXPERTS * FF, D), FF ** -0.5, 0.0625, ((0, 64), (1, 8)))
    gate_pre = normal_values(streams_of[4], (SLOTS, EXPERTS * FF), 1.0, 5.0, ((1, 512),))
    up_pre = normal_values(streams_of[5], (SLOTS, EXPERTS * FF), 1.0, 5.0, ((1, 512),))
    return {"grad_out": grad_out, "routes": routes, "gates": gates, "w_down": w_down, "gate_pre": gate_pre, "up_pre": up_pre}


def reference(grad_out, routes, gates, w_down, gate_pre, up_pre):
    pair_experts = routes.reshape(N_EXPERT, TOK_DEV * TOP)
    pair_tokens = jnp.repeat(jnp.arange(TOKENS, dtype=jnp.int32), TOP)
    pair_rows = grad_out[pair_tokens]
    gate_flat = gates.reshape(-1)
    plane_width = D // N_TENSOR
    source = jnp.arange(N_EXPERT, dtype=jnp.int32)[:, None]
    gate_grad = jnp.zeros((TOKENS * TOP,), jnp.float32)
    weight_parts = []
    gate_parts = []
    up_parts = []
    for expert in range(EXPERTS):
        matches = pair_experts == expert
        ranking = jnp.cumsum(matches.astype(jnp.int32), axis=1) - 1
        slot_index = jnp.where(matches, source * CAP + ranking, SLOTS).reshape(-1).astype(jnp.int32)
        slot_rows = jnp.zeros((SLOTS, D), jnp.bfloat16).at[slot_index].set(pair_rows, mode="drop")
        slot_gates = jnp.zeros((SLOTS,), jnp.bfloat16).at[slot_index].set(gate_flat, mode="drop").astype(jnp.float32)
        weight = w_down[expert * FF:(expert + 1) * FF]
        hidden_grad = jnp.zeros((SLOTS, FF), jnp.float32)
        for plane in range(N_TENSOR):
            lower = plane * plane_width
            plane_term = jnp.dot(slot_rows[:, lower:lower + plane_width],
                                 weight[:, lower:lower + plane_width].T,
                                 preferred_element_type=jnp.float32)
            hidden_grad = hidden_grad + lax.optimization_barrier(plane_term.astype(jnp.bfloat16)).astype(jnp.float32)
        gate_act = gate_pre[:, expert * FF:(expert + 1) * FF].astype(jnp.float32)
        up_act = up_pre[:, expert * FF:(expert + 1) * FF].astype(jnp.float32)
        logistic = jax.nn.sigmoid(gate_act)
        swish_out = gate_act * logistic
        hidden = swish_out * up_act
        scale = slot_gates[:, None]
        gate_parts.append((scale * hidden_grad * up_act * logistic * (1.0 + gate_act * (1.0 - logistic))).astype(jnp.bfloat16))
        up_parts.append((scale * hidden_grad * swish_out).astype(jnp.bfloat16))
        scaled_hidden = (scale * hidden).astype(jnp.bfloat16)
        weight_parts.append(jnp.dot(scaled_hidden.T, slot_rows, preferred_element_type=jnp.float32).astype(jnp.bfloat16))
        slot_dots = jnp.sum(hidden * hidden_grad, axis=1)
        picked = slot_dots[jnp.minimum(slot_index, SLOTS - 1)]
        gate_grad = gate_grad + jnp.where(slot_index < SLOTS, picked, jnp.float32(0.0))
    w_down_grad = jnp.concatenate(weight_parts, axis=0)
    gate_pre_grad = jnp.concatenate(gate_parts, axis=1)
    up_pre_grad = jnp.concatenate(up_parts, axis=1)
    return (w_down_grad, gate_pre_grad, up_pre_grad, gate_grad.reshape(TOKENS, TOP))
```

```python
import jax
import jax.numpy as jnp
from jax import lax
from jax.sharding import Mesh
from jax.sharding import PartitionSpec as P

EXPERTS = 8
CAP = 24
BF = jnp.bfloat16
F32 = jnp.float32


def shift(x, axis, step):
    n = lax.axis_size(axis)
    return lax.ppermute(x, axis, [(i, (i + step) % n) for i in range(n)])


def swap(x, axis, mask):
    n = lax.axis_size(axis)
    return lax.ppermute(x, axis, [(i, i ^ mask) for i in range(n)])


def per_device(grad_out, routes, gates, w_down, gate_pre, up_pre):
    ny, nz = lax.axis_size("y"), lax.axis_size("z")
    nx, nc = lax.axis_size("x"), lax.axis_size("c")
    zi, xi, ci = lax.axis_index("z"), lax.axis_index("x"), lax.axis_index("c")
    tokens, width = grad_out.shape
    fb = gate_pre.shape[1]
    block = ny * CAP
    slots = nz * block

    routes_t = routes.T
    gates_t = gates.T.astype(F32)
    named = routes_t[:, None, :] == jnp.arange(EXPERTS, dtype=jnp.int32)[None, :, None]
    member = jnp.any(named, axis=0)
    weight = jnp.sum(jnp.where(named, gates_t[:, None, :], 0.0), axis=0)
    earlier = (
        jnp.arange(tokens, dtype=jnp.int32)[:, None] < jnp.arange(tokens, dtype=jnp.int32)[None, :]
    )
    rank = jnp.dot(member.astype(BF), earlier.astype(BF), preferred_element_type=F32).astype(jnp.int32)
    chosen = member[:, None, :] & (rank[:, None, :] == jnp.arange(CAP, dtype=jnp.int32)[None, :, None])
    selector = jnp.where(chosen, weight[:, None, :], 0.0).astype(BF).reshape(EXPERTS * CAP, tokens)
    packed = jnp.dot(selector, grad_out, preferred_element_type=F32).astype(BF)

    own = lax.all_to_all(
        packed.reshape(EXPERTS, CAP, width), "y", split_axis=0, concat_axis=0, tiled=True
    ).reshape(block, width)
    ahead, behind = [own], [own]
    for _ in range(nz // 2 - 1):
        behind.append(shift(behind[-1], "z", 1))
        ahead.append(shift(ahead[-1], "z", -1))
    half = block // 2
    far_low = shift(behind[-1][:half], "z", 1)
    far_high = shift(ahead[-1][half:], "z", -1)
    rows = jnp.concatenate(ahead + [far_low, far_high] + behind[:0:-1], axis=0)

    def ring_order(a):
        a = a.reshape(ny, nz, CAP, a.shape[1]).transpose(1, 0, 2, 3)
        return jnp.roll(a, -zi, axis=0).reshape(slots, a.shape[3])

    def slot_order(a):
        a = jnp.roll(a.reshape(nz, ny, CAP, a.shape[1]), zi, axis=0)
        return a.transpose(1, 0, 2, 3).reshape(slots, a.shape[3])

    gate_act = ring_order(gate_pre).astype(F32)
    up_act = ring_order(up_pre).astype(F32)
    logistic = jax.nn.sigmoid(gate_act)
    swish_out = gate_act * logistic
    hidden = lax.all_gather((swish_out * up_act).astype(BF), ("x", "c"), axis=1, tiled=True)

    def units(i, j):
        return lax.dynamic_slice_in_dim(w_down, ((xi ^ i) * nc + (ci ^ j)) * fb, fb, 0)

    w_other = jnp.concatenate([units(i, 1) for i in range(nx)], axis=0)
    w_own = jnp.concatenate([units(i, 0) for i in range(nx)], axis=0)

    def product(w):
        return lax.dot_general(rows, w, (((1,), (1,)), ((), ())), preferred_element_type=F32)

    got = swap(product(w_other).astype(BF), "c", 1)
    part = product(w_own) + got.astype(F32)
    hs = slots // 2
    pa, pb = part[:hs], part[hs:]

    def cols(a, i, n=1):
        return a[:, i * fb : (i + n) * fb]

    ga = swap(cols(pa, 1, 2).astype(BF), "x", 1).astype(F32)
    gb = swap(cols(pb, 2, 2).astype(BF), "x", 3).astype(F32)
    qa0, qa3 = cols(pa, 0) + cols(ga, 0), cols(pa, 3) + cols(ga, 1)
    qb0, qb1 = cols(pb, 0) + cols(gb, 1), cols(pb, 1) + cols(gb, 0)
    ga = swap(qa3.astype(BF), "x", 3).astype(F32)
    gb = swap(qb1.astype(BF), "x", 1).astype(F32)
    hidden_grad = jnp.concatenate([qa0 + ga, qb0 + gb], axis=0)

    gate_pre_grad = slot_order(
        (hidden_grad * up_act * logistic * (1.0 + gate_act * (1.0 - logistic))).astype(BF)
    )
    up_pre_grad = slot_order((hidden_grad * swish_out).astype(BF))

    w_down_grad = lax.dot_general(
        hidden, rows, (((0,), (0,)), ((), ())), preferred_element_type=F32
    ).astype(BF)

    outputs = jnp.dot(hidden, w_down, preferred_element_type=F32)
    dots = jnp.sum(rows.astype(F32) * outputs, axis=1)
    dots = lax.psum(dots, ("x", "c"))
    dots = jnp.roll(dots.reshape(nz, ny, CAP), zi, axis=0).transpose(1, 0, 2)
    back = lax.all_to_all(
        dots.reshape(ny * nz, CAP), ("y", "z"), split_axis=0, concat_axis=0, tiled=True
    )
    totals = jnp.sum(back.reshape(EXPERTS, nz, CAP), axis=1)
    by_token = jnp.sum(jnp.where(chosen, totals[:, :, None], 0.0), axis=1)
    gate_grad = jnp.sum(jnp.where(named, by_token[None], 0.0), axis=1) / gates_t
    return (w_down_grad, gate_pre_grad, up_pre_grad, gate_grad.T)


def solution(mesh):
    fine = Mesh(
        mesh.devices.reshape(EXPERTS, mesh.shape["expert"] // EXPERTS, mesh.shape["tensor"] // 2, 2),
        ("y", "z", "x", "c"),
    )
    e, t = ("y", "z"), ("x", "c")
    return jax.shard_map(
        per_device,
        mesh=fine,
        in_specs=(P(e, t), P(e, None), P(e, None), P(e, t), P(None, e + t), P(None, e + t)),
        out_specs=(P(e, t), P(None, e + t), P(None, e + t), P(e, None)),
        check_vma=False,
    )
```

```python
import jax
import jax.numpy as jnp
from jax import lax
from jax.experimental import pallas as pl
from jax.experimental.pallas import tpu as pltpu
from jax.sharding import Mesh
from jax.sharding import PartitionSpec as P

EXPERTS = 8
CAP = 24
NZ = 8
NX = 4
BLOCK = EXPERTS * CAP
HALF = BLOCK // 2
SIZES = (HALF, BLOCK, BLOCK, BLOCK, HALF)
STARTS = (0, 96, 288, 480, 672)
MINE = 768
BF = jnp.bfloat16
F32 = jnp.float32
VM = pl.BlockSpec(memory_space=pltpu.VMEM)
SM = pl.BlockSpec(memory_space=pltpu.SMEM)


def call(body, outs, ins, cost):
    specs = [SM if a.dtype == jnp.int32 and a.shape == (40,) else VM for a in ins]
    return pl.pallas_call(
        body,
        out_shape=[jax.ShapeDtypeStruct(s, d) for s, d in outs],
        in_specs=specs,
        out_specs=[VM] * len(outs),
        compiler_params=pltpu.CompilerParams(vmem_limit_bytes=48 * 2**20),
        cost_estimate=pl.CostEstimate(flops=cost[0], bytes_accessed=cost[1], transcendentals=0),
    )(*ins)


def dot(a, b, da, db):
    return lax.dot_general(a, b, (((da,), (db,)), ((), ())), preferred_element_type=F32)


def pack_body(routes, gates, rows, out):
    tokens = rows.shape[0]
    expert = lax.broadcasted_iota(jnp.int32, (EXPERTS, tokens), 0)
    first, second = routes[0:1, :] == expert, routes[1:2, :] == expert
    weight = jnp.where(first, gates[0:1, :], 0.0) + jnp.where(second, gates[1:2, :], 0.0)
    member = jnp.where(first | second, 1.0, 0.0)
    at = lax.broadcasted_iota(jnp.int32, (tokens, tokens), 0)
    to = lax.broadcasted_iota(jnp.int32, (tokens, tokens), 1)
    earlier = jnp.where(at < to, 1.0, 0.0).astype(BF)
    rank = dot(member.astype(BF), earlier, 1, 0)
    rank = jnp.where(member > 0.0, rank, -1.0).astype(jnp.int32)
    place = lax.broadcasted_iota(jnp.int32, (CAP, tokens), 0)
    chosen = [
        jnp.where(rank[e : e + 1] == place, weight[e : e + 1], 0.0) for e in range(EXPERTS)
    ]
    out[...] = dot(jnp.concatenate(chosen, axis=0).astype(BF), rows[...], 1, 0).astype(BF)


def act_body(table, gate, up, mine, other, by_gate, by_up):
    for g in range(16):
        zs, half = table[g], table[16 + g]
        a = gate[pl.ds(half * 4, 4), zs].astype(F32).reshape(HALF, 128)
        b = up[pl.ds(half * 4, 4), zs].astype(F32).reshape(HALF, 128)
        sig = 1.0 / (1.0 + jnp.exp(-a))
        swish = a * sig
        at = pl.ds((g % 8) * HALF, HALF)
        (mine if g < 8 else other)[at, :] = (swish * b).astype(BF)
        by_gate[pl.ds(g * HALF, HALF), :] = b * sig * (1.0 + a * (1.0 - sig))
        by_up[pl.ds(g * HALF, HALF), :] = swish


def product_body(labels, table, r0, r1, r2, r3, r4, w_own, w_other, ha, hb, out, dots):
    ones = jnp.ones((8, 256), F32)
    core = table[36]
    first = pl.ds(pl.multiple_of(core * HALF, HALF), HALF)
    for piece, (ref, size, start) in enumerate(zip((r0, r1, r2, r3, r4), SIZES, STARTS)):
        rows = first if piece == 0 else pl.ds(0, size)
        own, other = ref[0, rows, :], ref[1, rows, :]
        total = None
        for i, h in enumerate((ha, hb)):
            at = pl.ds(pl.multiple_of(table[32 + labels[i]] * 256, 256), 256)
            part = dot(own, w_own[at, :], 1, 1) + dot(other, w_other[at, :], 1, 1)
            out[pl.ds(start, size), pl.ds(i * 256, 256)] = part.astype(out.dtype)
            term = part * h[pl.ds(start, size), :].astype(F32)
            total = term if total is None else total + term
        dots[:, pl.ds(start, size)] = lax.dot_general(
            ones, total, (((1,), (1,)), ((), ())), precision=lax.Precision.HIGHEST,
            preferred_element_type=F32,
        )


def weight_body(which, table, r0, r1, r2, r3, r4, h0, h1, h2, h3, *rest):
    out = rest[-1]
    core = table[36]
    first = pl.ds(pl.multiple_of(core * HALF, HALF), HALF)
    for label, h in enumerate((h0, h1, h2, h3)):
        total = None
        for piece, (ref, size, start) in enumerate(zip((r0, r1, r2, r3, r4), SIZES, STARTS)):
            rows = first if piece == 0 else pl.ds(0, size)
            term = dot(h[pl.ds(start, size), :], ref[which, rows, :], 0, 0)
            total = term if total is None else total + term
        at = pl.ds(pl.multiple_of(table[32 + label] * 256, 256), 256)
        if len(rest) == 2:
            total = total + rest[0][at, :].astype(F32)
        out[at, :] = total.astype(BF)


def grad_body(table, kept, got, by_gate, by_up, gate_out, up_out):
    for g in range(16):
        zs, half = table[g], table[16 + g]
        src = (kept if g < 8 else got)[pl.ds((g % 8) * HALF, HALF), :].astype(F32)
        at = pl.ds(g * HALF, HALF)
        gate_out[pl.ds(half * 4, 4), zs] = (src * by_gate[at, :]).reshape(4, CAP, 128).astype(BF)
        up_out[pl.ds(half * 4, 4), zs] = (src * by_up[at, :]).reshape(4, CAP, 128).astype(BF)


def per_device(grad_out, routes, gates, w_down, gate_pre, up_pre):
    zi, xi, ci = lax.axis_index("z"), lax.axis_index("x"), lax.axis_index("c")
    tokens, width = grad_out.shape
    ff = w_down.shape[0]

    sign = 2 * ci - 1
    m1, m2 = 1 + 2 * ci, 3 - 2 * ci
    steps = jnp.array([0, 1, 1, 2, 2, 3, 3, 4], jnp.int32)
    halves = jnp.array([0, 0, 1, 0, 1, 0, 1, 0], jnp.int32)
    ends = jnp.array([1, 0, 0, 0, 0, 0, 0, 1], jnp.int32)
    table = jnp.concatenate(
        [
            (zi + sign * steps) % NZ,
            (zi - sign * steps) % NZ,
            halves + ends * ci,
            halves + ends * (1 - ci),
            jnp.stack([xi, xi ^ m2, xi ^ m1, xi ^ 2, ci, ci, ci, ci]),
        ]
    ).astype(jnp.int32)

    def swap_core(x):
        return lax.ppermute(x, "c", [(0, 1), (1, 0)])

    def ring(x):
        return lax.ppermute(
            x, ("z", "c"), [(z * 2 + c, (z + 1 - 2 * c) % NZ * 2 + c) for z in range(NZ) for c in range(2)]
        )

    def swap_x(x, first):
        masks = (1, 3) if first else (3, 1)
        return lax.ppermute(
            x, ("x", "c"), [(i * 2 + c, (i ^ masks[c]) * 2 + c) for i in range(NX) for c in range(2)]
        )

    def pair(own, other):
        low, high = jnp.where(ci == 0, own, other), jnp.where(ci == 0, other, own)
        return jnp.concatenate([low, high], axis=1)

    routes_t, gates_t = routes.T, gates.T.astype(F32)
    (packed,) = call(
        pack_body, [((BLOCK, width), BF)], (routes_t, gates_t, grad_out), (2 * BLOCK * tokens * width, 400000)
    )
    own = lax.all_to_all(
        packed.reshape(EXPERTS, CAP, width), "y", split_axis=0, concat_axis=0, tiled=True
    ).reshape(BLOCK, width)
    w_other = swap_core(w_down)

    view = (EXPERTS, NZ, CAP, 128)
    mine, other, by_gate, by_up = call(
        act_body,
        [((MINE, 128), BF), ((MINE, 128), BF), ((2 * MINE, 128), F32), ((2 * MINE, 128), F32)],
        (table, gate_pre.reshape(view), up_pre.reshape(view)),
        (20 * 2 * MINE * 128, 3000000),
    )
    h0 = pair(mine, swap_core(other))
    h2 = swap_x(h0, True)
    h1 = swap_x(h0, False)
    h3 = swap_x(h2, False)

    r0 = jnp.stack([own, swap_core(own)])
    r1 = ring(r0)
    r2 = ring(r1)
    r3 = ring(r2)
    r4 = ring(lax.dynamic_slice_in_dim(r3, ci * HALF, HALF, 1))
    pieces = (r0, r1, r2, r3, r4)

    def product(labels, ha, hb, dtype):
        return call(
            lambda *refs: product_body(labels, *refs),
            [((MINE, 512), dtype), ((8, MINE), F32)],
            (table, *pieces, w_down, w_other, ha, hb),
            (2 * MINE * 512 * 2 * width, 6000000),
        )

    send, dots_a = product((2, 3), h2, h3, BF)
    keep, dots_b = product((0, 1), h0, h1, F32)
    part = keep + swap_x(send, True).astype(F32)
    whole = part[:, :256] + swap_x(part[:, 256:].astype(BF), False).astype(F32)
    low, high = whole[:, :128], whole[:, 128:]
    kept = jnp.where(ci == 0, low, high)
    got = swap_core(jnp.where(ci == 0, high, low).astype(BF))
    gate_pre_grad, up_pre_grad = call(
        grad_body, [(view, BF), (view, BF)], (table, kept, got, by_gate, by_up), (4 * MINE * 128, 3000000)
    )

    dots = (dots_a[0] + dots_b[0]).reshape(8, 4, CAP)
    zero = jnp.zeros((1, 4, CAP), F32)
    near = dots[1:7].reshape(3, EXPERTS, CAP)
    none = jnp.zeros_like(near)
    at0, at4 = dots[0:1], dots[7:8]

    def spread(c):
        ends = [jnp.concatenate([a, zero] if c == 0 else [zero, a], axis=1) for a in (at0, at4)]
        sides = (none, near[::-1]) if c == 0 else (near, none)
        return jnp.concatenate([ends[0], sides[0], ends[1], sides[1]], axis=0)

    by_source = jnp.roll(jnp.where(ci == 0, spread(0), spread(1)), zi, axis=0).transpose(1, 0, 2)
    back = lax.all_to_all(
        by_source.reshape(EXPERTS * NZ, CAP), ("y", "z"), split_axis=0, concat_axis=0, tiled=True
    )
    totals = jnp.sum(back.reshape(EXPERTS, NZ, CAP), axis=1)
    totals = totals + swap_core(totals)
    totals = totals + swap_x(totals, True)
    totals = totals + swap_x(totals, False)

    named = routes_t[:, None, :] == jnp.arange(EXPERTS, dtype=jnp.int32)[None, :, None]
    member = jnp.any(named, axis=0)
    order = jnp.arange(tokens, dtype=jnp.int32)
    earlier = (order[:, None] < order[None, :]).astype(BF)
    rank = jnp.dot(member.astype(BF), earlier, preferred_element_type=F32).astype(jnp.int32)
    chosen = member[:, None, :] & (rank[:, None, :] == jnp.arange(CAP, dtype=jnp.int32)[None, :, None])
    by_token = jnp.sum(jnp.where(chosen, totals[:, :, None], 0.0), axis=1)
    gate_grad = jnp.sum(jnp.where(named, by_token[None], 0.0), axis=1) / gates_t

    hiddens = (h0, h1, h2, h3)
    cost = (2 * MINE * ff * width, 5000000)
    (lent,) = call(
        lambda *refs: weight_body(1, *refs), [((ff, width), BF)], (table, *pieces, *hiddens), cost
    )
    (w_down_grad,) = call(
        lambda *refs: weight_body(0, *refs),
        [((ff, width), BF)],
        (table, *pieces, *hiddens, swap_core(lent)),
        cost,
    )
    flat = (EXPERTS * NZ * CAP, 128)
    return (w_down_grad, gate_pre_grad.reshape(flat), up_pre_grad.reshape(flat), gate_grad.T)


def solution(mesh):
    fine = Mesh(mesh.devices.reshape(EXPERTS, NZ, NX, 2), ("y", "z", "x", "c"))
    e, t = ("y", "z"), ("x", "c")
    return jax.shard_map(
        per_device,
        mesh=fine,
        in_specs=(P(e, t), P(e, None), P(e, None), P(e, t), P(None, e + t), P(None, e + t)),
        out_specs=(P(e, t), P(None, e + t), P(None, e + t), P(e, None)),
        check_vma=False,
    )
```

```python
import jax
import jax.numpy as jnp
from jax import lax
from jax.experimental import pallas as pl
from jax.experimental.pallas import tpu as pltpu
from jax.sharding import Mesh
from jax.sharding import PartitionSpec as P

EXPERTS = 8
CAP = 24
NZ = 8
NX = 4
BLOCK = EXPERTS * CAP
HALF = BLOCK // 2
SIZES = (HALF, BLOCK, BLOCK, BLOCK, HALF)
STARTS = (0, 96, 288, 480, 672)
MINE = 768
BF = jnp.bfloat16
F32 = jnp.float32
VM = pl.BlockSpec(memory_space=pltpu.VMEM)
SM = pl.BlockSpec(memory_space=pltpu.SMEM)


def call(body, outs, ins, cost, scratch=(), aliases={}):
    specs = [SM if a.dtype == jnp.int32 and a.shape == (40,) else VM for a in ins]
    return pl.pallas_call(
        body,
        out_shape=[jax.ShapeDtypeStruct(s, d) for s, d in outs],
        in_specs=specs,
        out_specs=[VM] * len(outs),
        scratch_shapes=[pltpu.VMEM(s, BF) for s in scratch],
        input_output_aliases=aliases,
        compiler_params=pltpu.CompilerParams(vmem_limit_bytes=48 * 2**20),
        cost_estimate=pl.CostEstimate(flops=cost[0], bytes_accessed=cost[1], transcendentals=0),
    )(*ins)


def dot(a, b, da, db):
    return lax.dot_general(a, b, (((da,), (db,)), ((), ())), preferred_element_type=F32)


def pack_body(routes, gates, rows, out):
    tokens = rows.shape[0]
    expert = lax.broadcasted_iota(jnp.int32, (EXPERTS, tokens), 0)
    first, second = routes[0:1, :] == expert, routes[1:2, :] == expert
    weight = jnp.where(first, gates[0:1, :], 0.0) + jnp.where(second, gates[1:2, :], 0.0)
    member = jnp.where(first | second, 1.0, 0.0)
    at = lax.broadcasted_iota(jnp.int32, (tokens, tokens), 0)
    to = lax.broadcasted_iota(jnp.int32, (tokens, tokens), 1)
    earlier = jnp.where(at < to, 1.0, 0.0).astype(BF)
    rank = dot(member.astype(BF), earlier, 1, 0)
    rank = jnp.where(member > 0.0, rank, -1.0).astype(jnp.int32)
    place = lax.broadcasted_iota(jnp.int32, (CAP, tokens), 0)
    chosen = [
        jnp.where(rank[e : e + 1] == place, weight[e : e + 1], 0.0) for e in range(EXPERTS)
    ]
    out[...] = dot(jnp.concatenate(chosen, axis=0).astype(BF), rows[...], 1, 0).astype(BF)


def act_body(table, gate, up, hidden, by_gate, by_up):
    core = table[36]
    for g in range(16):
        zs, half = table[g], table[16 + g]
        a = gate[pl.ds(half * 4, 4), zs].astype(F32).reshape(HALF, 128)
        b = up[pl.ds(half * 4, 4), zs].astype(F32).reshape(HALF, 128)
        sig = 1.0 / (1.0 + jnp.exp(-a))
        swish = a * sig
        hidden[core if g < 8 else 1 - core, pl.ds((g % 8) * HALF, HALF), :] = (swish * b).astype(BF)
        by_gate[pl.ds(g * HALF, HALF), :] = b * sig * (1.0 + a * (1.0 - sig))
        by_up[pl.ds(g * HALF, HALF), :] = swish


def half_of(core):
    return pl.ds(pl.multiple_of(core * HALF, HALF), HALF)


def product(table, own, other, w_own, w_other, hidden, start, send, keep, dots):
    core = table[36]
    size = own.shape[0]
    at = pl.ds(start, size)
    total = None
    for label in (2, 3, 0, 1):
        unit = table[32 + label]
        w = pl.ds(pl.multiple_of(unit * 256, 256), 256)
        part = dot(own[...], w_own[w, :], 1, 1) + dot(other[...], w_other[w, :], 1, 1)
        if label >= 2:
            send[at, pl.ds((label - 2) * 256, 256)] = part.astype(BF)
        else:
            keep[at, pl.ds(label * 256, 256)] = part
        for i in range(2):
            term = part[:, i * 128 : i * 128 + 128] * hidden[2 * unit + i, core, at, :].astype(F32)
            total = term if total is None else total + term
    dots[...] = lax.dot_general(
        jnp.ones((8, 128), F32), total, (((1,), (1,)), ((), ())),
        precision=lax.Precision.HIGHEST, preferred_element_type=F32,
    )


def near_body(table, r0, r1, r2, r3, w_own, w_other, hidden, send, keep, dots, own, other):
    core = table[36]
    for side, dst in enumerate((own, other)):
        dst[pl.ds(0, HALF), :] = r0[side, half_of(core), :]
        for piece, ref in enumerate((r1, r2, r3)):
            dst[pl.ds(STARTS[piece + 1], BLOCK), :] = ref[side]
    product(table, own, other, w_own, w_other, hidden, 0, send, keep, dots)


def far_body(table, r4, w_own, w_other, hidden, send_in, keep_in, send, keep, dots, own, other):
    del send_in, keep_in
    own[...] = r4[0]
    other[...] = r4[1]
    product(table, own, other, w_own, w_other, hidden, STARTS[4], send, keep, dots)


def weight_body(table, r0, r1, r2, r3, r4, lent, hidden, out, rows, units):
    core = table[36]
    rows[pl.ds(0, HALF), :] = r0[0, half_of(core), :]
    for ref, size, start in zip((r1, r2, r3, r4), SIZES[1:], STARTS[1:]):
        rows[pl.ds(start, size), :] = ref[0]
    rows[pl.ds(MINE, HALF), :] = r0[0, half_of(1 - core), :]
    rows[pl.ds(MINE + HALF, MINE - HALF), :] = lent[...]
    for pair in range(4):
        for i in range(2):
            lanes = pl.ds(i * 128, 128)
            units[pl.ds(0, MINE), lanes] = hidden[2 * pair + i, core]
            units[pl.ds(MINE, MINE), lanes] = hidden[2 * pair + i, 1 - core]
        out[pl.ds(pair * 256, 256), :] = dot(units[...], rows[...], 0, 0).astype(BF)


def grad_body(table, kept, got, by_gate, by_up, gate_out, up_out):
    for g in range(16):
        zs, half = table[g], table[16 + g]
        src = (kept if g < 8 else got)[pl.ds((g % 8) * HALF, HALF), :].astype(F32)
        at = pl.ds(g * HALF, HALF)
        gate_out[pl.ds(half * 4, 4), zs] = (src * by_gate[at, :]).reshape(4, CAP, 128).astype(BF)
        up_out[pl.ds(half * 4, 4), zs] = (src * by_up[at, :]).reshape(4, CAP, 128).astype(BF)


def per_device(grad_out, routes, gates, w_down, gate_pre, up_pre):
    zi, xi, ci = lax.axis_index("z"), lax.axis_index("x"), lax.axis_index("c")
    tokens, width = grad_out.shape
    ff = w_down.shape[0]

    sign = 2 * ci - 1
    m1, m2 = 1 + 2 * ci, 3 - 2 * ci
    steps = jnp.array([0, 1, 1, 2, 2, 3, 3, 4], jnp.int32)
    halves = jnp.array([0, 0, 1, 0, 1, 0, 1, 0], jnp.int32)
    ends = jnp.array([1, 0, 0, 0, 0, 0, 0, 1], jnp.int32)
    table = jnp.concatenate(
        [
            (zi + sign * steps) % NZ,
            (zi - sign * steps) % NZ,
            halves + ends * ci,
            halves + ends * (1 - ci),
            jnp.stack([xi, xi ^ m2, xi ^ m1, xi ^ 2, ci, ci, ci, ci]),
        ]
    ).astype(jnp.int32)

    def swap_core(x):
        return lax.ppermute(x, "c", [(0, 1), (1, 0)])

    def ring(x):
        return lax.ppermute(
            x, ("z", "c"), [(z * 2 + c, (z + 1 - 2 * c) % NZ * 2 + c) for z in range(NZ) for c in range(2)]
        )

    def swap_x(x, first):
        masks = (1, 3) if first else (3, 1)
        return lax.ppermute(
            x, ("x", "c"), [(i * 2 + c, (i ^ masks[c]) * 2 + c) for i in range(NX) for c in range(2)]
        )

    routes_t, gates_t = routes.T, gates.T.astype(F32)
    (packed,) = call(
        pack_body, [((BLOCK, width), BF)], (routes_t, gates_t, grad_out), (2 * BLOCK * tokens * width, 400000)
    )
    own = lax.all_to_all(
        packed.reshape(EXPERTS, CAP, width), "y", split_axis=0, concat_axis=0, tiled=True
    ).reshape(BLOCK, width)
    w_other = swap_core(w_down)

    view = (EXPERTS, NZ, CAP, 128)
    mine, by_gate, by_up = call(
        act_body,
        [((2, MINE, 128), BF), ((2 * MINE, 128), F32), ((2 * MINE, 128), F32)],
        (table, gate_pre.reshape(view), up_pre.reshape(view)),
        (20 * 2 * MINE * 128, 3000000),
    )
    hidden = lax.all_gather(mine, ("x", "c"), axis=0)

    own, w_other, mine = lax.optimization_barrier((own, w_other, mine))
    r0 = jnp.stack([own, swap_core(own)])
    r1 = ring(r0)
    r2 = ring(r1)
    r3 = ring(r2)
    r4 = ring(lax.dynamic_slice_in_dim(r3, ci * HALF, HALF, 1))

    outs = [((MINE, 512), BF), ((MINE, 512), F32)]
    send, keep, dots_a = call(
        near_body,
        outs + [((8, STARTS[4]), F32)],
        (table, r0, r1, r2, r3, w_down, w_other, hidden),
        (2 * MINE * ff * 2 * width, 9000000),
        ((STARTS[4], width),) * 2,
    )
    send, keep, dots_b = call(
        far_body,
        outs + [((8, HALF), F32)],
        (table, r4, w_down, w_other, hidden, send, keep),
        (2 * HALF * ff * 2 * width, 6000000),
        ((HALF, width),) * 2,
        {5: 0, 6: 1},
    )
    part = keep + swap_x(send, True).astype(F32)
    whole = part[:, :256] + swap_x(part[:, 256:].astype(BF), False).astype(F32)
    low, high = whole[:, :128], whole[:, 128:]
    kept = jnp.where(ci == 0, low, high)
    got = swap_core(jnp.where(ci == 0, high, low).astype(BF))
    gate_pre_grad, up_pre_grad = call(
        grad_body, [(view, BF), (view, BF)], (table, kept, got, by_gate, by_up), (4 * MINE * 128, 3000000)
    )

    dots = jnp.concatenate([dots_a[0], dots_b[0]]).reshape(8, 4, CAP)
    zero = jnp.zeros((1, 4, CAP), F32)
    near = dots[1:7].reshape(3, EXPERTS, CAP)
    none = jnp.zeros_like(near)
    at0, at4 = dots[0:1], dots[7:8]

    def spread(c):
        ends = [jnp.concatenate([a, zero] if c == 0 else [zero, a], axis=1) for a in (at0, at4)]
        sides = (none, near[::-1]) if c == 0 else (near, none)
        return jnp.concatenate([ends[0], sides[0], ends[1], sides[1]], axis=0)

    by_source = jnp.roll(jnp.where(ci == 0, spread(0), spread(1)), zi, axis=0).transpose(1, 0, 2)
    back = lax.all_to_all(
        by_source.reshape(EXPERTS * NZ, CAP), ("y", "z"), split_axis=0, concat_axis=0, tiled=True
    )
    totals = jnp.sum(back.reshape(EXPERTS, NZ, CAP), axis=1)
    totals = totals + swap_core(totals)
    totals = totals + swap_x(totals, True)
    totals = totals + swap_x(totals, False)

    named = routes_t[:, None, :] == jnp.arange(EXPERTS, dtype=jnp.int32)[None, :, None]
    member = jnp.any(named, axis=0)
    order = jnp.arange(tokens, dtype=jnp.int32)
    earlier = (order[:, None] < order[None, :]).astype(BF)
    rank = jnp.dot(member.astype(BF), earlier, preferred_element_type=F32).astype(jnp.int32)
    chosen = member[:, None, :] & (rank[:, None, :] == jnp.arange(CAP, dtype=jnp.int32)[None, :, None])
    by_token = jnp.sum(jnp.where(chosen, totals[:, :, None], 0.0), axis=1)
    gate_grad = jnp.sum(jnp.where(named, by_token[None], 0.0), axis=1) / gates_t

    lent = swap_core(jnp.concatenate([r1[1], r2[1], r3[1], r4[1]], axis=0))
    (w_down_grad,) = call(
        weight_body,
        [((ff, width), BF)],
        (table, r0, r1, r2, r3, r4, lent, hidden),
        (2 * 2 * MINE * ff * width, 9000000),
        ((2 * MINE, width), (2 * MINE, 256)),
    )
    flat = (EXPERTS * NZ * CAP, 128)
    return (w_down_grad, gate_pre_grad.reshape(flat), up_pre_grad.reshape(flat), gate_grad.T)


def solution(mesh):
    fine = Mesh(mesh.devices.reshape(EXPERTS, NZ, NX, 2), ("y", "z", "x", "c"))
    e, t = ("y", "z"), ("x", "c")
    return jax.shard_map(
        per_device,
        mesh=fine,
        in_specs=(P(e, t), P(e, None), P(e, None), P(e, t), P(None, e + t), P(None, e + t)),
        out_specs=(P(e, t), P(None, e + t), P(None, e + t), P(e, None)),
        check_vma=False,
    )
```

```python
import jax
import jax.numpy as jnp
from jax import lax
from jax.experimental import pallas as pl
from jax.experimental.pallas import tpu as pltpu
from jax.sharding import Mesh
from jax.sharding import PartitionSpec as P

EXPERTS = 8
CAP = 24
NZ = 8
NX = 4
BLOCK = EXPERTS * CAP
HALF = BLOCK // 2
NEAR = 5 * HALF
FAR = 3 * HALF
MINE = 768
BF = jnp.bfloat16
F32 = jnp.float32
VM = pl.BlockSpec()
SM = pl.BlockSpec(memory_space=pltpu.SMEM)


def call(body, outs, ins, cost, scratch=(), limit=40):
    specs = [SM if a.dtype == jnp.int32 and a.shape == (3,) else VM for a in ins]
    return pl.pallas_call(
        body,
        out_shape=[jax.ShapeDtypeStruct(s, d) for s, d in outs],
        in_specs=specs,
        out_specs=[VM] * len(outs),
        scratch_shapes=[pltpu.VMEM(s, BF) for s in scratch],
        compiler_params=pltpu.CompilerParams(vmem_limit_bytes=limit * 2**20),
        cost_estimate=pl.CostEstimate(flops=cost[0], bytes_accessed=cost[1], transcendentals=0),
    )(*ins)


def dot(a, b, da, db):
    return lax.dot_general(a, b, (((da,), (db,)), ((), ())), preferred_element_type=F32)


def pack_body(routes, gates_ref, rows, out):
    gates = gates_ref[...].astype(F32)
    tokens = rows.shape[0]
    expert = lax.broadcasted_iota(jnp.int32, (EXPERTS, tokens), 0)
    first, second = routes[0:1, :] == expert, routes[1:2, :] == expert
    weight = jnp.where(first, gates[0:1, :], 0.0) + jnp.where(second, gates[1:2, :], 0.0)
    member = jnp.where(first | second, 1.0, 0.0)
    at = lax.broadcasted_iota(jnp.int32, (tokens, tokens), 0)
    to = lax.broadcasted_iota(jnp.int32, (tokens, tokens), 1)
    earlier = jnp.where(at < to, 1.0, 0.0).astype(BF)
    rank = dot(member.astype(BF), earlier, 1, 0)
    rank = jnp.where(member > 0.0, rank, -1.0).astype(jnp.int32)
    place = lax.broadcasted_iota(jnp.int32, (CAP, tokens), 0)
    chosen = [
        jnp.where(rank[e : e + 1] == place, weight[e : e + 1], 0.0) for e in range(EXPERTS)
    ]
    out[...] = dot(jnp.concatenate(chosen, axis=0).astype(BF), rows[...], 1, 0).astype(BF)


STEPS = (0, 1, 1, 2, 2, 3, 3, 4)
FLIPS = (0, 0, 1, 0, 1, 0, 1, 0)


def group(place, g):
    core = place[2] if g < 8 else 1 - place[2]
    step = STEPS[g % 8]
    return (place[0] + NZ + (2 * core - 1) * step) % NZ, core ^ FLIPS[g % 8]


def unit_of(place, label):
    first = 1 + 2 * place[2]
    masks = (0, 4 - first, first, 2)
    return place[1] ^ masks[label]


def act_body(table, gate, up, hidden):
    core = table[2]
    for g in range(16):
        zs, half = group(table, g)
        a = gate[pl.ds(half * 4, 4), zs].astype(F32).reshape(HALF, 128)
        b = up[pl.ds(half * 4, 4), zs].astype(F32).reshape(HALF, 128)
        sig = 1.0 / (1.0 + jnp.exp(-a))
        hidden[core if g < 8 else 1 - core, pl.ds((g % 8) * HALF, HALF), :] = (a * sig * b).astype(BF)


def product_body(count, start, table, *refs):
    pieces, (w_own, w_other, hidden, send, keep, dots, own, other) = refs[:count], refs[count:]
    core = table[2]
    size = count * HALF
    for piece, ref in enumerate(pieces):
        own[pl.ds(piece * HALF, HALF), :] = ref[0]
        other[pl.ds(piece * HALF, HALF), :] = ref[1]
    total = None
    for label in (2, 3, 0, 1):
        unit = unit_of(table, label)
        w = pl.ds(pl.multiple_of(unit * 256, 256), 256)
        part = dot(own[...], w_own[w, :], 1, 1) + dot(other[...], w_other[w, :], 1, 1)
        if label >= 2:
            send[:, pl.ds((label - 2) * 256, 256)] = part.astype(BF)
        else:
            keep[:, pl.ds(label * 256, 256)] = part
        for i in range(2):
            h = hidden[2 * unit + i, core, pl.ds(start, size), :]
            term = part[:, i * 128 : i * 128 + 128] * h.astype(F32)
            total = term if total is None else total + term
    dots[...] = lax.dot_general(
        jnp.ones((8, 128), F32), total, (((1,), (1,)), ((), ())),
        precision=lax.Precision.HIGHEST, preferred_element_type=F32,
    )


def weight_body(table, *refs):
    pieces, (spare, lent, hidden, out, rows, units) = refs[:8], refs[8:]
    core = table[2]
    for piece, ref in enumerate(pieces):
        rows[pl.ds(piece * HALF, HALF), :] = ref[0]
    rows[pl.ds(MINE, HALF), :] = spare[0]
    rows[pl.ds(MINE + HALF, MINE - HALF), :] = lent[...]
    for pair in range(4):
        for i in range(2):
            lanes = pl.ds(i * 128, 128)
            units[pl.ds(0, MINE), lanes] = hidden[2 * pair + i, core]
            units[pl.ds(MINE, MINE), lanes] = hidden[2 * pair + i, 1 - core]
        out[pl.ds(pair * 256, 256), :] = dot(units[...], rows[...], 0, 0).astype(BF)


def grad_body(table, kept, got, gate, up, gate_out, up_out):
    for g in range(16):
        zs, half = group(table, g)
        planes = pl.ds(half * 4, 4)
        src = (kept if g < 8 else got)[pl.ds((g % 8) * HALF, HALF), :].astype(F32).reshape(4, CAP, 128)
        a, b = gate[planes, zs].astype(F32), up[planes, zs].astype(F32)
        sig = 1.0 / (1.0 + jnp.exp(-a))
        gate_out[planes, zs] = (src * b * sig * (1.0 + a * (1.0 - sig))).astype(BF)
        up_out[planes, zs] = (src * (a * sig)).astype(BF)


def per_device(grad_out, routes, gates, w_down, gate_pre, up_pre):
    zi, xi, ci = lax.axis_index("z"), lax.axis_index("x"), lax.axis_index("c")
    tokens, width = grad_out.shape
    ff = w_down.shape[0]

    table = jnp.stack([zi, xi, ci]).astype(jnp.int32)

    def after(x, *others):
        return lax.optimization_barrier((x, *others))[0]

    def swap_core(x):
        return lax.ppermute(x, "c", [(0, 1), (1, 0)])

    def ring(x):
        return lax.ppermute(
            x, ("z", "c"), [(z * 2 + c, (z + 1 - 2 * c) % NZ * 2 + c) for z in range(NZ) for c in range(2)]
        )

    def swap_x(x, first):
        masks = (1, 3) if first else (3, 1)
        return lax.ppermute(
            x, ("x", "c"), [(i * 2 + c, (i ^ masks[c]) * 2 + c) for i in range(NX) for c in range(2)]
        )

    routes_t, gates_t = routes.T, gates.T
    (packed,) = call(
        pack_body, [((BLOCK, width), BF)], (routes_t, gates_t, grad_out), (2 * BLOCK * tokens * width, 400000)
    )
    own = lax.all_to_all(
        packed.reshape(EXPERTS, CAP, width), "y", split_axis=0, concat_axis=0, tiled=True
    ).reshape(BLOCK, width)
    view = (EXPERTS, NZ, CAP, 128)
    gate_view, up_view = gate_pre.reshape(view), up_pre.reshape(view)
    (mine,) = call(
        act_body, [((2, MINE, 128), BF)], (table, gate_view, up_view), (20 * 2 * MINE * 128, 2000000)
    )
    hidden = lax.all_gather(mine, ("x", "c"), axis=0)

    sides = jnp.stack([own, swap_core(own)])
    ra = [lax.dynamic_slice_in_dim(sides, ci * HALF, HALF, 1)]
    rb = [lax.dynamic_slice_in_dim(sides, (1 - ci) * HALF, HALF, 1)]
    for step in range(3):
        ra.append(ring(ra[-1]))
        rb.append(ring(rb[-1]))
    w_other = swap_core(after(w_down, ra[1]))

    def product(pieces, start):
        size = len(pieces) * HALF
        return call(
            lambda *refs: product_body(len(pieces), start, *refs),
            [((size, 512), BF), ((size, 512), F32), ((8, size), F32)],
            (table, *pieces, w_down, w_other, hidden),
            (2 * size * ff * 2 * width, 9000000),
            ((size, width),) * 2,
        )

    send, keep, dots_near = product((ra[0], ra[1], rb[1], ra[2], rb[2]), 0)
    ra.append(ring(after(ra[3], send)))
    part = keep + swap_x(send, True).astype(F32)
    near = part[:, :256] + swap_x(part[:, 256:].astype(BF), False).astype(F32)
    send, keep, dots_far = product((ra[3], rb[3], after(ra[4], near)), NEAR)
    part = keep + swap_x(send, True).astype(F32)
    last = part[:, 256:].astype(BF)
    far = part[:, :256] + swap_x(last, False).astype(F32)
    pieces = (ra[0], ra[1], rb[1], ra[2], rb[2], ra[3], rb[3], ra[4])
    whole = jnp.concatenate([near, far], axis=0)
    low, high = whole[:, :128], whole[:, 128:]
    kept = jnp.where(ci == 0, low, high)
    got = swap_core(jnp.where(ci == 0, high, low).astype(BF))
    gate_pre_grad, up_pre_grad = call(
        grad_body, [(view, BF), (view, BF)], (table, kept, got, gate_view, up_view), (4 * MINE * 128, 3000000)
    )

    dots = jnp.concatenate([dots_near[0], dots_far[0]]).reshape(8, 4, CAP)
    zero = jnp.zeros((1, 4, CAP), F32)
    sides_of = dots[1:7].reshape(3, 2, 4, CAP)
    none = jnp.zeros((3, EXPERTS, CAP), F32)
    at0, at4 = dots[0:1], dots[7:8]

    def spread(c):
        ends = [jnp.concatenate([a, zero] if c == 0 else [zero, a], axis=1) for a in (at0, at4)]
        flat = (sides_of if c == 0 else sides_of[:, ::-1]).reshape(3, EXPERTS, CAP)
        sides = (none, flat[::-1]) if c == 0 else (flat, none)
        return jnp.concatenate([ends[0], sides[0], ends[1], sides[1]], axis=0)

    by_source = jnp.roll(jnp.where(ci == 0, spread(0), spread(1)), zi, axis=0).transpose(1, 0, 2)
    back = lax.all_to_all(
        by_source.reshape(EXPERTS * NZ, CAP), ("y", "z"), split_axis=0, concat_axis=0, tiled=True
    )
    totals = jnp.sum(back.reshape(EXPERTS, NZ, CAP), axis=1)
    totals = totals + swap_core(totals)
    totals = totals + swap_x(totals, True)
    totals = totals + swap_x(totals, False)

    named = routes_t[:, None, :] == jnp.arange(EXPERTS, dtype=jnp.int32)[None, :, None]
    member = jnp.any(named, axis=0)
    order = jnp.arange(tokens, dtype=jnp.int32)
    earlier = (order[:, None] < order[None, :]).astype(BF)
    rank = jnp.dot(member.astype(BF), earlier, preferred_element_type=F32).astype(jnp.int32)
    chosen = member[:, None, :] & (rank[:, None, :] == jnp.arange(CAP, dtype=jnp.int32)[None, :, None])
    by_token = jnp.sum(jnp.where(chosen, totals[:, :, None], 0.0), axis=1)
    gate_grad = jnp.sum(jnp.where(named, by_token[None], 0.0), axis=1) / gates_t.astype(F32)

    lent = swap_core(jnp.concatenate([piece[1] for piece in pieces[1:]], axis=0))
    (w_down_grad,) = call(
        weight_body,
        [((ff, width), BF)],
        (table, *pieces, rb[0], after(lent, last), hidden),
        (2 * 2 * MINE * ff * width, 9000000),
        ((2 * MINE, width), (2 * MINE, 256)),
    )
    flat = (EXPERTS * NZ * CAP, 128)
    return (w_down_grad, gate_pre_grad.reshape(flat), up_pre_grad.reshape(flat), gate_grad.T)


def solution(mesh):
    fine = Mesh(mesh.devices.reshape(EXPERTS, NZ, NX, 2), ("y", "z", "x", "c"))
    e, t = ("y", "z"), ("x", "c")
    return jax.shard_map(
        per_device,
        mesh=fine,
        in_specs=(P(e, t), P(e, None), P(e, None), P(e, t), P(None, e + t), P(None, e + t)),
        out_specs=(P(e, t), P(None, e + t), P(None, e + t), P(e, None)),
        check_vma=False,
    )
```

```python
import jax
import jax.numpy as jnp
from jax import lax
from jax.experimental import pallas as pl
from jax.experimental.pallas import tpu as pltpu
from jax.sharding import Mesh
from jax.sharding import PartitionSpec as P

EXPERTS = 8
CAP = 24
NZ = 8
NX = 4
BLOCK = EXPERTS * CAP
SLOTS = NZ * BLOCK
PART = SLOTS // 2
BF = jnp.bfloat16
F32 = jnp.float32
WHOLE = pl.BlockSpec()
SM = pl.BlockSpec(memory_space=pltpu.SMEM)


def call(body, outs, ins, cost, scratch=()):
    specs = [SM if a.dtype == jnp.int32 and a.shape == (2,) else WHOLE for a in ins]
    return pl.pallas_call(
        body,
        out_shape=[jax.ShapeDtypeStruct(s, d) for s, d in outs],
        in_specs=specs,
        out_specs=[WHOLE] * len(outs),
        scratch_shapes=scratch,
        compiler_params=pltpu.CompilerParams(vmem_limit_bytes=40 * 2**20),
        cost_estimate=pl.CostEstimate(flops=cost[0], bytes_accessed=cost[1], transcendentals=0),
    )(*ins)


def dot(a, b, da, db):
    return lax.dot_general(a, b, (((da,), (db,)), ((), ())), preferred_element_type=F32)


def pack_body(routes, gates_ref, rows, out):
    gates = gates_ref[...].astype(F32)
    tokens = rows.shape[0]
    expert = lax.broadcasted_iota(jnp.int32, (EXPERTS, tokens), 0)
    first, second = routes[0:1, :] == expert, routes[1:2, :] == expert
    weight = jnp.where(first, gates[0:1, :], 0.0) + jnp.where(second, gates[1:2, :], 0.0)
    member = jnp.where(first | second, 1.0, 0.0)
    at = lax.broadcasted_iota(jnp.int32, (tokens, tokens), 0)
    to = lax.broadcasted_iota(jnp.int32, (tokens, tokens), 1)
    earlier = jnp.where(at < to, 1.0, 0.0).astype(BF)
    rank = dot(member.astype(BF), earlier, 1, 0)
    rank = jnp.where(member > 0.0, rank, -1.0).astype(jnp.int32)
    place = lax.broadcasted_iota(jnp.int32, (CAP, tokens), 0)
    chosen = [
        jnp.where(rank[e : e + 1] == place, weight[e : e + 1], 0.0) for e in range(EXPERTS)
    ]
    out[...] = dot(jnp.concatenate(chosen, axis=0).astype(BF), rows[...], 1, 0).astype(BF)


def act_body(gate, up, hidden):
    for z in range(NZ):
        a = gate[:, z].astype(F32).reshape(BLOCK, 128)
        b = up[:, z].astype(F32).reshape(BLOCK, 128)
        sig = 1.0 / (1.0 + jnp.exp(-a))
        hidden[z // 4, pl.ds(z % 4 * BLOCK, BLOCK), :] = (a * sig * b).astype(BF)


def product_body(rows, w, out):
    part = dot(rows[...], w[...], 1, 1).astype(BF)
    out[0] = part[:, :128]
    out[1] = part[:, 128:]


def hidden_blocks(place, refs):
    masks = (0, 3 - 2 * place[1], 1 + 2 * place[1], 2)
    lent = refs[4]
    for label in range(4):
        yield place[0] ^ masks[label], refs[label], lent[(0, 2, 1, 3)[label]]


def slots_of(core):
    return pl.ds(pl.multiple_of(core * PART, PART), PART)


def dots_body(place, parts, h0, h1, h2, h3, lent, dots, total):
    core = place[1]
    mine, others = slots_of(core), slots_of(1 - core)
    total[...] = jnp.zeros_like(total)
    for x, own, got in hidden_blocks(place, (h0, h1, h2, h3, lent)):
        for i in range(2):
            total[mine, :] += parts[2 * x + i, mine, :].astype(F32) * own[i].astype(F32)
            total[others, :] += parts[2 * x + i, others, :].astype(F32) * got[i].astype(F32)
    dots[...] = lax.dot_general(
        jnp.ones((8, 128), F32), total[...], (((1,), (1,)), ((), ())),
        precision=lax.Precision.HIGHEST, preferred_element_type=F32,
    )


def weight_body(place, rows, h0, h1, h2, h3, lent, out, units):
    core = place[1]
    mine, others = slots_of(core), slots_of(1 - core)
    for x, own, got in hidden_blocks(place, (h0, h1, h2, h3, lent)):
        for i in range(2):
            units[mine, pl.ds(i * 128, 128)] = own[i]
            units[others, pl.ds(i * 128, 128)] = got[i]
        at = pl.ds(pl.multiple_of(x * 256, 256), 256)
        out[at, :] = dot(units[...], rows[...], 0, 0).astype(BF)


def grad_body(hidden_grad, gate, up, gate_out, up_out):
    for z in range(NZ):
        src = hidden_grad[pl.ds(z * BLOCK, BLOCK), :].astype(F32).reshape(EXPERTS, CAP, 128)
        a, b = gate[:, z].astype(F32), up[:, z].astype(F32)
        sig = 1.0 / (1.0 + jnp.exp(-a))
        gate_out[:, z] = (src * b * sig * (1.0 + a * (1.0 - sig))).astype(BF)
        up_out[:, z] = (src * (a * sig)).astype(BF)


def per_device(grad_out, routes, gates, w_down, gate_pre, up_pre):
    xi, ci = lax.axis_index("x"), lax.axis_index("c")
    tokens, width = grad_out.shape
    ff = w_down.shape[0]
    place = jnp.stack([xi, ci]).astype(jnp.int32)

    def swap_core(x):
        return lax.ppermute(x, "c", [(0, 1), (1, 0)])

    def swap_x(x, first):
        masks = (1, 3) if first else (3, 1)
        return lax.ppermute(
            x, ("x", "c"), [(i * 2 + c, (i ^ masks[c]) * 2 + c) for i in range(NX) for c in range(2)]
        )

    routes_t, gates_t = routes.T, gates.T
    (packed,) = call(
        pack_body, [((BLOCK, width), BF)], (routes_t, gates_t, grad_out), (2 * BLOCK * tokens * width, 400000)
    )
    own = lax.all_to_all(
        packed.reshape(EXPERTS, CAP, width), "y", split_axis=0, concat_axis=0, tiled=True
    ).reshape(BLOCK, width)
    rows = lax.all_gather(own, "z", axis=0, tiled=True)

    view = (EXPERTS, NZ, CAP, 128)
    gate_late, up_late, _ = lax.optimization_barrier((gate_pre, up_pre, own))
    gate_view, up_view = gate_late.reshape(view), up_late.reshape(view)
    (hid,) = call(
        act_body, [((2, PART, 128), BF)], (gate_view, up_view), (20 * SLOTS * 128, 2000000)
    )
    keep = lax.dynamic_index_in_dim(hid, ci, 0, keepdims=False)
    got = swap_core(lax.dynamic_index_in_dim(hid, 1 - ci, 0, keepdims=False))
    h0 = jnp.stack([jnp.where(ci == 0, keep, got), jnp.where(ci == 0, got, keep)])
    h2 = swap_x(h0, True)
    h1 = swap_x(h0, False)
    h3 = swap_x(h2, False)
    lent = swap_core(jnp.stack([h0, h1, h2, h3]))
    rows, lent = lax.optimization_barrier((rows, lent))
    hiddens = (h0, h1, h2, h3, lent)

    parts = pl.pallas_call(
        product_body,
        grid=(NX,),
        out_shape=jax.ShapeDtypeStruct((2 * NX, SLOTS, 128), BF),
        in_specs=[
            pl.BlockSpec((SLOTS, width), lambda i: (0, 0)),
            pl.BlockSpec((ff // NX, width), lambda i: (i, 0)),
        ],
        out_specs=pl.BlockSpec((2, SLOTS, 128), lambda i: (i, 0, 0)),
        compiler_params=pltpu.CompilerParams(vmem_limit_bytes=40 * 2**20),
        cost_estimate=pl.CostEstimate(
            flops=2 * SLOTS * ff * width, bytes_accessed=8000000, transcendentals=0
        ),
    )(rows, w_down)
    hidden_grad = lax.psum_scatter(parts, ("x", "c"), scatter_dimension=0)
    gate_pre_grad, up_pre_grad = call(
        grad_body, [(view, BF), (view, BF)], (hidden_grad, gate_view, up_view), (4 * SLOTS * 128, 3000000)
    )

    (dots,) = call(
        dots_body,
        [((8, SLOTS), F32)],
        (place, parts, *hiddens),
        (2 * SLOTS * ff, 6000000),
        (pltpu.VMEM((SLOTS, 128), F32),),
    )
    back = lax.all_to_all(
        dots[0].reshape(NZ * EXPERTS, CAP), ("z", "y"), split_axis=0, concat_axis=0, tiled=True
    )
    totals = jnp.sum(back.reshape(NZ, EXPERTS, CAP), axis=0)
    totals = totals + swap_core(totals)
    totals = totals + swap_x(totals, True)
    totals = totals + swap_x(totals, False)

    named = routes_t[:, None, :] == jnp.arange(EXPERTS, dtype=jnp.int32)[None, :, None]
    member = jnp.any(named, axis=0)
    order = jnp.arange(tokens, dtype=jnp.int32)
    earlier = (order[:, None] < order[None, :]).astype(BF)
    rank = jnp.dot(member.astype(BF), earlier, preferred_element_type=F32).astype(jnp.int32)
    chosen = member[:, None, :] & (rank[:, None, :] == jnp.arange(CAP, dtype=jnp.int32)[None, :, None])
    by_token = jnp.sum(jnp.where(chosen, totals[:, :, None], 0.0), axis=1)
    gate_grad = jnp.sum(jnp.where(named, by_token[None], 0.0), axis=1) / gates_t.astype(F32)

    (w_down_grad,) = call(
        weight_body,
        [((ff, width), BF)],
        (place, rows, *hiddens),
        (2 * SLOTS * ff * width, 9000000),
        (pltpu.VMEM((SLOTS, 256), BF),),
    )
    flat = (EXPERTS * NZ * CAP, 128)
    return (w_down_grad, gate_pre_grad.reshape(flat), up_pre_grad.reshape(flat), gate_grad.T)


def solution(mesh):
    fine = Mesh(mesh.devices.reshape(EXPERTS, NZ, NX, 2), ("y", "z", "x", "c"))
    e, t = ("y", "z"), ("x", "c")
    return jax.shard_map(
        per_device,
        mesh=fine,
        in_specs=(P(e, t), P(e, None), P(e, None), P(e, t), P(None, e + t), P(None, e + t)),
        out_specs=(P(e, t), P(None, e + t), P(None, e + t), P(e, None)),
        check_vma=False,
    )
```

```python
import jax
import jax.numpy as jnp
from jax import lax
from jax.experimental import pallas as pl
from jax.experimental.pallas import tpu as pltpu
from jax.sharding import Mesh
from jax.sharding import PartitionSpec as P

EXPERTS = 8
CAP = 24
NZ = 8
NX = 4
BLOCK = EXPERTS * CAP
SLOTS = NZ * BLOCK
PART = SLOTS // 2
BF = jnp.bfloat16
F32 = jnp.float32
LIMIT = 52 * 2**20
WHOLE = pl.BlockSpec()
CHUNK = SLOTS // 4


def call(body, outs, ins, cost):
    return pl.pallas_call(
        body,
        out_shape=[jax.ShapeDtypeStruct(s, d) for s, d in outs],
        in_specs=[WHOLE] * len(ins),
        out_specs=[WHOLE] * len(outs),
        compiler_params=pltpu.CompilerParams(vmem_limit_bytes=LIMIT),
        cost_estimate=pl.CostEstimate(flops=cost[0], bytes_accessed=cost[1], transcendentals=0),
    )(*ins)


def dot(a, b, da, db):
    return lax.dot_general(a, b, (((da,), (db,)), ((), ())), preferred_element_type=F32)


def pack_body(routes, gates_ref, rows, out):
    gates = gates_ref[...].astype(F32)
    tokens = rows.shape[0]
    expert = lax.broadcasted_iota(jnp.int32, (EXPERTS, tokens), 0)
    first, second = routes[0:1, :] == expert, routes[1:2, :] == expert
    weight = jnp.where(first, gates[0:1, :], 0.0) + jnp.where(second, gates[1:2, :], 0.0)
    member = jnp.where(first | second, 1.0, 0.0)
    at = lax.broadcasted_iota(jnp.int32, (tokens, tokens), 0)
    to = lax.broadcasted_iota(jnp.int32, (tokens, tokens), 1)
    earlier = jnp.where(at < to, 1.0, 0.0).astype(BF)
    rank = dot(member.astype(BF), earlier, 1, 0)
    rank = jnp.where(member > 0.0, rank, -1.0).astype(jnp.int32)
    place = lax.broadcasted_iota(jnp.int32, (CAP, tokens), 0)
    chosen = [
        jnp.where(rank[e : e + 1] == place, weight[e : e + 1], 0.0) for e in range(EXPERTS)
    ]
    out[...] = dot(jnp.concatenate(chosen, axis=0).astype(BF), rows[...], 1, 0).astype(BF)


def act_body(gate, up, hidden):
    for z in range(NZ):
        a = gate[:, z].astype(F32).reshape(BLOCK, 128)
        b = up[:, z].astype(F32).reshape(BLOCK, 128)
        sig = 1.0 / (1.0 + jnp.exp(-a))
        hidden[z // 4, pl.ds(z % 4 * BLOCK, BLOCK), :] = (a * sig * b).astype(BF)


def x_of(label, place):
    mask = jnp.where(label == 1, 3 - 2 * place[1], jnp.where(label == 2, 1 + 2 * place[1], label - label // 3))
    return place[0] ^ mask


def swapped(label):
    return jnp.where(label == 1, 2, jnp.where(label == 2, 1, label))


def product_body(place, rows, w, mine, lent, parts, dots, total):
    label = pl.program_id(0)

    @pl.when(label == 0)
    def _():
        total[...] = jnp.zeros_like(total)

    for k in range(4):
        at = pl.ds(k * CHUNK, CHUNK)
        part = dot(rows[at, :], w[...], 1, 1)
        here = pl.ds(k % 2 * CHUNK, CHUNK)
        for i in range(2):
            unit = part[:, i * 128 : i * 128 + 128]
            parts[i, at, :] = unit.astype(BF)
            hidden = jnp.where(place[1] == k // 2, mine[0, i, here, :], lent[0, i, here, :])
            total[at, :] += unit * hidden.astype(F32)

    @pl.when(label == NX - 1)
    def _():
        dots[...] = lax.dot_general(
            jnp.ones((8, 128), F32), total[...], (((1,), (1,)), ((), ())),
            precision=lax.Precision.HIGHEST, preferred_element_type=F32,
        )


def weight_body(place, rows, mine, lent, out, units):
    for half in range(2):
        for i in range(2):
            hidden = jnp.where(place[1] == half, mine[0, i], lent[0, i])
            units[pl.ds(half * PART, PART), pl.ds(i * 128, 128)] = hidden
    out[...] = dot(units[...], rows[...], 0, 0).astype(BF)


def grad_body(hidden_grad, gate, up, gate_out, up_out):
    for z in range(NZ):
        src = hidden_grad[pl.ds(z * BLOCK, BLOCK), :].astype(F32).reshape(EXPERTS, CAP, 128)
        a, b = gate[:, z].astype(F32), up[:, z].astype(F32)
        sig = 1.0 / (1.0 + jnp.exp(-a))
        gate_out[:, z] = (src * b * sig * (1.0 + a * (1.0 - sig))).astype(BF)
        up_out[:, z] = (src * (a * sig)).astype(BF)


def per_device(grad_out, routes, gates, w_down, gate_pre, up_pre):
    xi, ci = lax.axis_index("x"), lax.axis_index("c")
    tokens, width = grad_out.shape
    ff = w_down.shape[0]
    place = jnp.stack([xi, ci]).astype(jnp.int32)

    def swap_core(x):
        return lax.ppermute(x, "c", [(0, 1), (1, 0)])

    def swap_x(x, first):
        masks = (1, 3) if first else (3, 1)
        return lax.ppermute(
            x, ("x", "c"), [(i * 2 + c, (i ^ masks[c]) * 2 + c) for i in range(NX) for c in range(2)]
        )

    routes_t, gates_t = routes.T, gates.T
    (packed,) = call(
        pack_body, [((BLOCK, width), BF)], (routes_t, gates_t, grad_out), (2 * BLOCK * tokens * width, 400000)
    )
    own = lax.all_to_all(
        packed.reshape(EXPERTS, CAP, width), "y", split_axis=0, concat_axis=0, tiled=True
    ).reshape(BLOCK, width)
    rows = lax.all_gather(own, "z", axis=0, tiled=True)

    view = (EXPERTS, NZ, CAP, 128)
    gate_late, up_late, _ = lax.optimization_barrier((gate_pre, up_pre, own))
    gate_view, up_view = gate_late.reshape(view), up_late.reshape(view)
    (hid,) = call(
        act_body, [((2, PART, 128), BF)], (gate_view, up_view), (20 * SLOTS * 128, 2000000)
    )
    keep = lax.dynamic_index_in_dim(hid, ci, 0, keepdims=False)
    got = swap_core(lax.dynamic_index_in_dim(hid, 1 - ci, 0, keepdims=False))
    h0 = jnp.stack([jnp.where(ci == 0, keep, got), jnp.where(ci == 0, got, keep)])
    h2 = swap_x(h0, True)
    h1 = swap_x(h0, False)
    h3 = swap_x(h2, False)
    mine = jnp.stack([h0, h1, h2, h3])
    lent = swap_core(mine)
    rows, lent = lax.optimization_barrier((rows, lent))

    hidden_specs = [
        pl.BlockSpec((1, 2, PART, 128), lambda i, place: (i, 0, 0, 0)),
        pl.BlockSpec((1, 2, PART, 128), lambda i, place: (swapped(i), 0, 0, 0)),
    ]
    rows_spec = pl.BlockSpec((SLOTS, width), lambda i, place: (0, 0))
    units_spec = pl.BlockSpec((ff // NX, width), lambda i, place: (x_of(i, place), 0))
    parts, dots = pl.pallas_call(
        product_body,
        out_shape=[
            jax.ShapeDtypeStruct((2 * NX, SLOTS, 128), BF),
            jax.ShapeDtypeStruct((8, SLOTS), F32),
        ],
        grid_spec=pltpu.PrefetchScalarGridSpec(
            num_scalar_prefetch=1,
            grid=(NX,),
            in_specs=[rows_spec, units_spec, *hidden_specs],
            out_specs=[
                pl.BlockSpec((2, SLOTS, 128), lambda i, place: (x_of(i, place), 0, 0)),
                pl.BlockSpec((8, SLOTS), lambda i, place: (0, 0)),
            ],
            scratch_shapes=[pltpu.VMEM((SLOTS, 128), F32)],
        ),
        compiler_params=pltpu.CompilerParams(vmem_limit_bytes=LIMIT),
        cost_estimate=pl.CostEstimate(
            flops=2 * SLOTS * ff * width, bytes_accessed=11000000, transcendentals=0
        ),
    )(place, rows, w_down, mine, lent)
    hidden_grad = lax.psum_scatter(parts, ("x", "c"), scatter_dimension=0)
    gate_pre_grad, up_pre_grad = call(
        grad_body, [(view, BF), (view, BF)], (hidden_grad, gate_view, up_view), (4 * SLOTS * 128, 3000000)
    )

    back = lax.all_to_all(
        dots[0].reshape(NZ * EXPERTS, CAP), ("z", "y"), split_axis=0, concat_axis=0, tiled=True
    )
    totals = jnp.sum(back.reshape(NZ, EXPERTS, CAP), axis=0)
    totals = totals + swap_core(totals)
    totals = totals + swap_x(totals, True)
    totals = totals + swap_x(totals, False)

    named = routes_t[:, None, :] == jnp.arange(EXPERTS, dtype=jnp.int32)[None, :, None]
    member = jnp.any(named, axis=0)
    order = jnp.arange(tokens, dtype=jnp.int32)
    earlier = (order[:, None] < order[None, :]).astype(BF)
    rank = jnp.dot(member.astype(BF), earlier, preferred_element_type=F32).astype(jnp.int32)
    chosen = member[:, None, :] & (rank[:, None, :] == jnp.arange(CAP, dtype=jnp.int32)[None, :, None])
    by_token = jnp.sum(jnp.where(chosen, totals[:, :, None], 0.0), axis=1)
    gate_grad = jnp.sum(jnp.where(named, by_token[None], 0.0), axis=1) / gates_t.astype(F32)

    w_down_grad = pl.pallas_call(
        weight_body,
        out_shape=jax.ShapeDtypeStruct((ff, width), BF),
        grid_spec=pltpu.PrefetchScalarGridSpec(
            num_scalar_prefetch=1,
            grid=(NX,),
            in_specs=[rows_spec, *hidden_specs],
            out_specs=units_spec,
            scratch_shapes=[pltpu.VMEM((SLOTS, 256), BF)],
        ),
        compiler_params=pltpu.CompilerParams(vmem_limit_bytes=LIMIT),
        cost_estimate=pl.CostEstimate(
            flops=2 * SLOTS * ff * width, bytes_accessed=8000000, transcendentals=0
        ),
    )(place, rows, mine, lent)
    flat = (EXPERTS * NZ * CAP, 128)
    return (w_down_grad, gate_pre_grad.reshape(flat), up_pre_grad.reshape(flat), gate_grad.T)


def solution(mesh):
    fine = Mesh(mesh.devices.reshape(EXPERTS, NZ, NX, 2), ("y", "z", "x", "c"))
    e, t = ("y", "z"), ("x", "c")
    return jax.shard_map(
        per_device,
        mesh=fine,
        in_specs=(P(e, t), P(e, None), P(e, None), P(e, t), P(None, e + t), P(None, e + t)),
        out_specs=(P(e, t), P(None, e + t), P(None, e + t), P(e, None)),
        check_vma=False,
    )
```

```python
import jax
import jax.numpy as jnp
from jax import lax
from jax.experimental import pallas as pl
from jax.experimental.pallas import tpu as pltpu
from jax.sharding import Mesh
from jax.sharding import PartitionSpec as P

EXPERTS = 8
CAP = 24
NZ = 8
NX = 4
BLOCK = EXPERTS * CAP
SLOTS = NZ * BLOCK
PART = SLOTS // 2
BF = jnp.bfloat16
F32 = jnp.float32
LIMIT = 52 * 2**20
STREAM_LIMIT = 56 * 2**20
WHOLE = pl.BlockSpec()
SCALARS = pl.BlockSpec(memory_space=pltpu.SMEM)
LOCAL = pl.BlockSpec(memory_space=pltpu.VMEM)
REMOTE = pl.BlockSpec(memory_space=pl.ANY)
CHUNK = SLOTS // 4


def call(body, outs, ins, cost):
    return pl.pallas_call(
        body,
        out_shape=[jax.ShapeDtypeStruct(s, d) for s, d in outs],
        in_specs=[WHOLE] * len(ins),
        out_specs=[WHOLE] * len(outs),
        compiler_params=pltpu.CompilerParams(vmem_limit_bytes=LIMIT),
        cost_estimate=pl.CostEstimate(flops=cost[0], bytes_accessed=cost[1], transcendentals=0),
    )(*ins)


def dot(a, b, da, db):
    return lax.dot_general(a, b, (((da,), (db,)), ((), ())), preferred_element_type=F32)


def pack_body(routes, gates_ref, rows, out):
    gates = gates_ref[...].astype(F32)
    tokens = rows.shape[0]
    expert = lax.broadcasted_iota(jnp.int32, (EXPERTS, tokens), 0)
    first, second = routes[0:1, :] == expert, routes[1:2, :] == expert
    weight = jnp.where(first, gates[0:1, :], 0.0) + jnp.where(second, gates[1:2, :], 0.0)
    member = jnp.where(first | second, 1.0, 0.0)
    at = lax.broadcasted_iota(jnp.int32, (tokens, tokens), 0)
    to = lax.broadcasted_iota(jnp.int32, (tokens, tokens), 1)
    earlier = jnp.where(at < to, 1.0, 0.0).astype(BF)
    rank = dot(member.astype(BF), earlier, 1, 0)
    rank = jnp.where(member > 0.0, rank, -1.0).astype(jnp.int32)
    place = lax.broadcasted_iota(jnp.int32, (CAP, tokens), 0)
    chosen = [
        jnp.where(rank[e : e + 1] == place, weight[e : e + 1], 0.0) for e in range(EXPERTS)
    ]
    out[...] = dot(jnp.concatenate(chosen, axis=0).astype(BF), rows[...], 1, 0).astype(BF)


def act_body(gate, up, hidden):
    for z in range(NZ):
        a = gate[:, z].astype(F32).reshape(BLOCK, 128)
        b = up[:, z].astype(F32).reshape(BLOCK, 128)
        sig = 1.0 / (1.0 + jnp.exp(-a))
        hidden[z // 4, pl.ds(z % 4 * BLOCK, BLOCK), :] = (a * sig * b).astype(BF)


def x_of(label, place):
    return place[0] ^ (0, 3 - 2 * place[1], 1 + 2 * place[1], 2)[label]


def hidden_of(place, mine, lent, label, half, i, at):
    return jnp.where(place[1] == half, mine[label, i, at, :], lent[OTHERS[label], i, at, :])


OTHERS = (0, 2, 1, 3)


def fetch(source, target, sems, size):
    copies = []
    for k in range(4):
        at = pl.ds(k * size, size)
        copies.append(pltpu.make_async_copy(source.at[at], target.at[at], sems.at[k]))
        copies[-1].start()
    return copies


def product_body(
    place, rows_in, w_in, mine_in, lent_in, parts_out, dots, rows, w, mine, lent, parts,
    in_sems, w_sems, mine_sems, lent_sems, out_sems,
):
    arriving = fetch(rows_in, rows, in_sems, CHUNK)
    units = fetch(w_in, w, w_sems, w.shape[0] // 4)
    ours = fetch(mine_in, mine, mine_sems, 1)
    coming = fetch(lent_in, lent, lent_sems, 1)
    for copy in units:
        copy.wait()
    leaving = []
    for k in range(4):
        at = pl.ds(k * CHUNK, CHUNK)
        here = pl.ds(k % 2 * CHUNK, CHUNK)
        arriving[k].wait()
        total = None
        for label in range(NX):
            x = x_of(label, place)
            part = dot(rows[at, :], w[pl.ds(pl.multiple_of(x * 256, 256), 256), :], 1, 1)
            if k == 0:
                ours[label].wait()
                coming[OTHERS[label]].wait()
            for i in range(2):
                unit = part[:, i * 128 : i * 128 + 128]
                slot = 2 * label + i
                parts[slot, at, :] = unit.astype(BF)
                copy = pltpu.make_async_copy(
                    parts.at[slot, at], parts_out.at[2 * x + i, at], out_sems.at[k, slot]
                )
                copy.start()
                leaving.append(copy)
                term = unit * hidden_of(place, mine, lent, label, k // 2, i, here).astype(F32)
                total = term if total is None else total + term
        dots[:, at] = lax.dot_general(
            jnp.ones((8, 128), F32), total, (((1,), (1,)), ((), ())),
            precision=lax.Precision.HIGHEST, preferred_element_type=F32,
        )
    for copy in leaving:
        copy.wait()


def weight_body(
    place, rows_in, mine_in, lent_in, out, rows, mine, lent, units, blocks,
    in_sems, mine_sems, lent_sems, out_sems,
):
    ours = fetch(mine_in, mine, mine_sems, 1)
    coming = fetch(lent_in, lent, lent_sems, 1)
    arriving = fetch(rows_in, rows, in_sems, CHUNK)
    leaving = []
    whole = pl.ds(0, PART)
    for label in range(NX):
        ours[label].wait()
        coming[OTHERS[label]].wait()
        for half in range(2):
            for i in range(2):
                units[label % 2, pl.ds(half * PART, PART), pl.ds(i * 128, 128)] = hidden_of(
                    place, mine, lent, label, half, i, whole
                )
        if label == 0:
            for copy in arriving:
                copy.wait()
        blocks[label] = dot(units[label % 2], rows[...], 0, 0).astype(BF)
        at = pl.ds(pl.multiple_of(x_of(label, place) * 256, 256), 256)
        leaving.append(pltpu.make_async_copy(blocks.at[label], out.at[at], out_sems.at[label]))
        leaving[-1].start()
    for copy in leaving:
        copy.wait()


def grad_body(hidden_grad, gate, up, gate_out, up_out):
    for z in range(NZ):
        src = hidden_grad[pl.ds(z * BLOCK, BLOCK), :].astype(F32).reshape(EXPERTS, CAP, 128)
        a, b = gate[:, z].astype(F32), up[:, z].astype(F32)
        sig = 1.0 / (1.0 + jnp.exp(-a))
        gate_out[:, z] = (src * b * sig * (1.0 + a * (1.0 - sig))).astype(BF)
        up_out[:, z] = (src * (a * sig)).astype(BF)


def per_device(grad_out, routes, gates, w_down, gate_pre, up_pre):
    xi, ci = lax.axis_index("x"), lax.axis_index("c")
    tokens, width = grad_out.shape
    ff = w_down.shape[0]
    place = jnp.stack([xi, ci]).astype(jnp.int32)

    def swap_core(x):
        return lax.ppermute(x, "c", [(0, 1), (1, 0)])

    def swap_x(x, first):
        masks = (1, 3) if first else (3, 1)
        return lax.ppermute(
            x, ("x", "c"), [(i * 2 + c, (i ^ masks[c]) * 2 + c) for i in range(NX) for c in range(2)]
        )

    routes_t, gates_t = routes.T, gates.T
    (packed,) = call(
        pack_body, [((BLOCK, width), BF)], (routes_t, gates_t, grad_out), (2 * BLOCK * tokens * width, 400000)
    )
    own = lax.all_to_all(
        packed.reshape(EXPERTS, CAP, width), "y", split_axis=0, concat_axis=0, tiled=True
    ).reshape(BLOCK, width)
    rows = lax.all_gather(own, "z", axis=0, tiled=True)

    view = (EXPERTS, NZ, CAP, 128)
    gate_late, up_late, _ = lax.optimization_barrier((gate_pre, up_pre, own))
    gate_view, up_view = gate_late.reshape(view), up_late.reshape(view)
    (hid,) = call(
        act_body, [((2, PART, 128), BF)], (gate_view, up_view), (20 * SLOTS * 128, 2000000)
    )
    keep = lax.dynamic_index_in_dim(hid, ci, 0, keepdims=False)
    got = swap_core(lax.dynamic_index_in_dim(hid, 1 - ci, 0, keepdims=False))
    h0 = jnp.stack([jnp.where(ci == 0, keep, got), jnp.where(ci == 0, got, keep)])
    h2 = swap_x(h0, True)
    h1 = swap_x(h0, False)
    h3 = swap_x(h2, False)
    mine = jnp.stack([h0, h1, h2, h3])
    lent = swap_core(mine)
    rows, lent = lax.optimization_barrier((rows, lent))

    parts, dots = pl.pallas_call(
        product_body,
        out_shape=[
            jax.ShapeDtypeStruct((2 * NX, SLOTS, 128), BF),
            jax.ShapeDtypeStruct((8, SLOTS), F32),
        ],
        in_specs=[SCALARS, REMOTE, REMOTE, REMOTE, REMOTE],
        out_specs=[REMOTE, LOCAL],
        scratch_shapes=[
            pltpu.VMEM((SLOTS, width), BF),
            pltpu.VMEM((ff, width), BF),
            pltpu.VMEM((NX, 2, PART, 128), BF),
            pltpu.VMEM((NX, 2, PART, 128), BF),
            pltpu.VMEM((2 * NX, SLOTS, 128), BF),
            pltpu.SemaphoreType.DMA((4,)),
            pltpu.SemaphoreType.DMA((4,)),
            pltpu.SemaphoreType.DMA((4,)),
            pltpu.SemaphoreType.DMA((4,)),
            pltpu.SemaphoreType.DMA((4, 2 * NX)),
        ],
        compiler_params=pltpu.CompilerParams(vmem_limit_bytes=STREAM_LIMIT),
        cost_estimate=pl.CostEstimate(
            flops=2 * SLOTS * ff * width, bytes_accessed=11000000, transcendentals=0
        ),
    )(place, rows, w_down, mine, lent)
    hidden_grad = lax.psum_scatter(parts, ("x", "c"), scatter_dimension=0)
    gate_pre_grad, up_pre_grad = call(
        grad_body, [(view, BF), (view, BF)], (hidden_grad, gate_view, up_view), (4 * SLOTS * 128, 3000000)
    )

    back = lax.all_to_all(
        dots[0].reshape(NZ * EXPERTS, CAP), ("z", "y"), split_axis=0, concat_axis=0, tiled=True
    )
    totals = jnp.sum(back.reshape(NZ, EXPERTS, CAP), axis=0)
    totals = totals + swap_core(totals)
    totals = totals + swap_x(totals, True)
    totals = totals + swap_x(totals, False)

    named = routes_t[:, None, :] == jnp.arange(EXPERTS, dtype=jnp.int32)[None, :, None]
    member = jnp.any(named, axis=0)
    order = jnp.arange(tokens, dtype=jnp.int32)
    earlier = (order[:, None] < order[None, :]).astype(BF)
    rank = jnp.dot(member.astype(BF), earlier, preferred_element_type=F32).astype(jnp.int32)
    chosen = member[:, None, :] & (rank[:, None, :] == jnp.arange(CAP, dtype=jnp.int32)[None, :, None])
    by_token = jnp.sum(jnp.where(chosen, totals[:, :, None], 0.0), axis=1)
    gate_grad = jnp.sum(jnp.where(named, by_token[None], 0.0), axis=1) / gates_t.astype(F32)

    w_down_grad = pl.pallas_call(
        weight_body,
        out_shape=jax.ShapeDtypeStruct((ff, width), BF),
        in_specs=[SCALARS, REMOTE, REMOTE, REMOTE],
        out_specs=REMOTE,
        scratch_shapes=[
            pltpu.VMEM((SLOTS, width), BF),
            pltpu.VMEM((NX, 2, PART, 128), BF),
            pltpu.VMEM((NX, 2, PART, 128), BF),
            pltpu.VMEM((2, SLOTS, 256), BF),
            pltpu.VMEM((NX, 256, width), BF),
            pltpu.SemaphoreType.DMA((4,)),
            pltpu.SemaphoreType.DMA((4,)),
            pltpu.SemaphoreType.DMA((4,)),
            pltpu.SemaphoreType.DMA((NX,)),
        ],
        compiler_params=pltpu.CompilerParams(vmem_limit_bytes=STREAM_LIMIT),
        cost_estimate=pl.CostEstimate(
            flops=2 * SLOTS * ff * width, bytes_accessed=8000000, transcendentals=0
        ),
    )(place, rows, mine, lent)
    flat = (EXPERTS * NZ * CAP, 128)
    return (w_down_grad, gate_pre_grad.reshape(flat), up_pre_grad.reshape(flat), gate_grad.T)


def solution(mesh):
    fine = Mesh(mesh.devices.reshape(EXPERTS, NZ, NX, 2), ("y", "z", "x", "c"))
    e, t = ("y", "z"), ("x", "c")
    return jax.shard_map(
        per_device,
        mesh=fine,
        in_specs=(P(e, t), P(e, None), P(e, None), P(e, t), P(None, e + t), P(None, e + t)),
        out_specs=(P(e, t), P(None, e + t), P(None, e + t), P(e, None)),
        check_vma=False,
    )
```

```python
import jax
import jax.numpy as jnp
from jax import lax
from jax.experimental import pallas as pl
from jax.experimental.pallas import tpu as pltpu
from jax.sharding import Mesh
from jax.sharding import PartitionSpec as P

EXPERTS = 8
CAP = 24
NZ = 8
NX = 4
BLOCK = EXPERTS * CAP
SLOTS = NZ * BLOCK
PART = SLOTS // 2
BF = jnp.bfloat16
F32 = jnp.float32
LIMIT = 24 * 2**20
WHOLE = pl.BlockSpec()
CHUNK = SLOTS // 4


def call(body, outs, ins, cost):
    return pl.pallas_call(
        body,
        out_shape=[jax.ShapeDtypeStruct(s, d) for s, d in outs],
        in_specs=[WHOLE] * len(ins),
        out_specs=[WHOLE] * len(outs),
        compiler_params=pltpu.CompilerParams(vmem_limit_bytes=LIMIT),
        cost_estimate=pl.CostEstimate(flops=cost[0], bytes_accessed=cost[1], transcendentals=0),
    )(*ins)


def dot(a, b, da, db):
    return lax.dot_general(a, b, (((da,), (db,)), ((), ())), preferred_element_type=F32)


def pack_body(routes, gates_ref, rows, out):
    gates = gates_ref[...].astype(F32)
    tokens = rows.shape[0]
    expert = lax.broadcasted_iota(jnp.int32, (EXPERTS, tokens), 0)
    first, second = routes[0:1, :] == expert, routes[1:2, :] == expert
    weight = jnp.where(first, gates[0:1, :], 0.0) + jnp.where(second, gates[1:2, :], 0.0)
    member = jnp.where(first | second, 1.0, 0.0)
    at = lax.broadcasted_iota(jnp.int32, (tokens, tokens), 0)
    to = lax.broadcasted_iota(jnp.int32, (tokens, tokens), 1)
    earlier = jnp.where(at < to, 1.0, 0.0).astype(BF)
    rank = dot(member.astype(BF), earlier, 1, 0)
    rank = jnp.where(member > 0.0, rank, -1.0).astype(jnp.int32)
    place = lax.broadcasted_iota(jnp.int32, (CAP, tokens), 0)
    chosen = [
        jnp.where(rank[e : e + 1] == place, weight[e : e + 1], 0.0) for e in range(EXPERTS)
    ]
    out[...] = dot(jnp.concatenate(chosen, axis=0).astype(BF), rows[...], 1, 0).astype(BF)


def act_body(gate, up, hidden):
    for z in range(NZ):
        a = gate[:, z].astype(F32).reshape(BLOCK, 128)
        b = up[:, z].astype(F32).reshape(BLOCK, 128)
        sig = 1.0 / (1.0 + jnp.exp(-a))
        hidden[z // 4, pl.ds(z % 4 * BLOCK, BLOCK), :] = (a * sig * b).astype(BF)


def x_of(label, place):
    mask = jnp.where(label == 1, 3 - 2 * place[1], jnp.where(label == 2, 1 + 2 * place[1], label - label // 3))
    return place[0] ^ mask


def swapped(label):
    return jnp.where(label == 1, 2, jnp.where(label == 2, 1, label))


def product_body(place, rows, w, mine, lent, parts, dots, total):
    label = pl.program_id(0)

    @pl.when(label == 0)
    def _():
        total[...] = jnp.zeros_like(total)

    for k in range(4):
        at = pl.ds(k * CHUNK, CHUNK)
        part = dot(rows[at, :], w[...], 1, 1)
        here = pl.ds(k % 2 * CHUNK, CHUNK)
        for i in range(2):
            unit = part[:, i * 128 : i * 128 + 128]
            parts[i, at, :] = unit.astype(BF)
            hidden = jnp.where(place[1] == k // 2, mine[0, i, here, :], lent[0, i, here, :])
            total[at, :] += unit * hidden.astype(F32)

    @pl.when(label == NX - 1)
    def _():
        dots[...] = lax.dot_general(
            jnp.ones((8, 128), F32), total[...], (((1,), (1,)), ((), ())),
            precision=lax.Precision.HIGHEST, preferred_element_type=F32,
        )


def weight_body(place, rows, mine, lent, out, units):
    for half in range(2):
        for i in range(2):
            hidden = jnp.where(place[1] == half, mine[0, i], lent[0, i])
            units[pl.ds(half * PART, PART), pl.ds(i * 128, 128)] = hidden
    out[...] = dot(units[...], rows[...], 0, 0).astype(BF)


def grad_body(hidden_grad, gate, up, gate_out, up_out):
    for z in range(NZ):
        src = hidden_grad[pl.ds(z * BLOCK, BLOCK), :].astype(F32).reshape(EXPERTS, CAP, 128)
        a, b = gate[:, z].astype(F32), up[:, z].astype(F32)
        sig = 1.0 / (1.0 + jnp.exp(-a))
        gate_out[:, z] = (src * b * sig * (1.0 + a * (1.0 - sig))).astype(BF)
        up_out[:, z] = (src * (a * sig)).astype(BF)


def per_device(grad_out, routes, gates, w_down, gate_pre, up_pre):
    xi, ci = lax.axis_index("x"), lax.axis_index("c")
    tokens, width = grad_out.shape
    ff = w_down.shape[0]
    place = jnp.stack([xi, ci]).astype(jnp.int32)

    def swap_core(x):
        return lax.ppermute(x, "c", [(0, 1), (1, 0)])

    def swap_x(x, first):
        masks = (1, 3) if first else (3, 1)
        return lax.ppermute(
            x, ("x", "c"), [(i * 2 + c, (i ^ masks[c]) * 2 + c) for i in range(NX) for c in range(2)]
        )

    routes_t, gates_t = routes.T, gates.T
    (packed,) = call(
        pack_body, [((BLOCK, width), BF)], (routes_t, gates_t, grad_out), (2 * BLOCK * tokens * width, 400000)
    )
    own = lax.all_to_all(
        packed.reshape(EXPERTS, CAP, width), "y", split_axis=0, concat_axis=0, tiled=True
    ).reshape(BLOCK, width)
    rows = lax.all_gather(own, "z", axis=0, tiled=True)

    view = (EXPERTS, NZ, CAP, 128)
    gate_late, up_late, _ = lax.optimization_barrier((gate_pre, up_pre, own))
    gate_view, up_view = gate_late.reshape(view), up_late.reshape(view)
    (hid,) = call(
        act_body, [((2, PART, 128), BF)], (gate_view, up_view), (20 * SLOTS * 128, 2000000)
    )
    keep = lax.dynamic_index_in_dim(hid, ci, 0, keepdims=False)
    got = swap_core(lax.dynamic_index_in_dim(hid, 1 - ci, 0, keepdims=False))
    h0 = jnp.stack([jnp.where(ci == 0, keep, got), jnp.where(ci == 0, got, keep)])
    h2 = swap_x(h0, True)
    h1 = swap_x(h0, False)
    h3 = swap_x(h2, False)
    mine = jnp.stack([h0, h1, h2, h3])
    lent = swap_core(mine)
    rows, lent = lax.optimization_barrier((rows, lent))

    hidden_specs = [
        pl.BlockSpec((1, 2, PART, 128), lambda i, place: (i, 0, 0, 0)),
        pl.BlockSpec((1, 2, PART, 128), lambda i, place: (swapped(i), 0, 0, 0)),
    ]
    rows_spec = pl.BlockSpec((SLOTS, width), lambda i, place: (0, 0))
    units_spec = pl.BlockSpec((ff // NX, width), lambda i, place: (x_of(i, place), 0))
    parts, dots = pl.pallas_call(
        product_body,
        out_shape=[
            jax.ShapeDtypeStruct((2 * NX, SLOTS, 128), BF),
            jax.ShapeDtypeStruct((8, SLOTS), F32),
        ],
        grid_spec=pltpu.PrefetchScalarGridSpec(
            num_scalar_prefetch=1,
            grid=(NX,),
            in_specs=[rows_spec, units_spec, *hidden_specs],
            out_specs=[
                pl.BlockSpec((2, SLOTS, 128), lambda i, place: (x_of(i, place), 0, 0)),
                pl.BlockSpec((8, SLOTS), lambda i, place: (0, 0)),
            ],
            scratch_shapes=[pltpu.VMEM((SLOTS, 128), F32)],
        ),
        compiler_params=pltpu.CompilerParams(vmem_limit_bytes=LIMIT),
        cost_estimate=pl.CostEstimate(
            flops=2 * SLOTS * ff * width, bytes_accessed=11000000, transcendentals=0
        ),
    )(place, rows, w_down, mine, lent)
    hidden_grad = lax.psum_scatter(parts, ("x", "c"), scatter_dimension=0)
    gate_pre_grad, up_pre_grad = call(
        grad_body, [(view, BF), (view, BF)], (hidden_grad, gate_view, up_view), (4 * SLOTS * 128, 3000000)
    )

    back = lax.all_to_all(
        dots[0].reshape(NZ * EXPERTS, CAP), ("z", "y"), split_axis=0, concat_axis=0, tiled=True
    )
    totals = jnp.sum(back.reshape(NZ, EXPERTS, CAP), axis=0)
    totals = totals + swap_core(totals)
    totals = totals + swap_x(totals, True)
    totals = totals + swap_x(totals, False)

    named = routes_t[:, None, :] == jnp.arange(EXPERTS, dtype=jnp.int32)[None, :, None]
    member = jnp.any(named, axis=0)
    order = jnp.arange(tokens, dtype=jnp.int32)
    earlier = (order[:, None] < order[None, :]).astype(BF)
    rank = jnp.dot(member.astype(BF), earlier, preferred_element_type=F32).astype(jnp.int32)
    chosen = member[:, None, :] & (rank[:, None, :] == jnp.arange(CAP, dtype=jnp.int32)[None, :, None])
    by_token = jnp.sum(jnp.where(chosen, totals[:, :, None], 0.0), axis=1)
    gate_grad = jnp.sum(jnp.where(named, by_token[None], 0.0), axis=1) / gates_t.astype(F32)

    w_down_grad = pl.pallas_call(
        weight_body,
        out_shape=jax.ShapeDtypeStruct((ff, width), BF),
        grid_spec=pltpu.PrefetchScalarGridSpec(
            num_scalar_prefetch=1,
            grid=(NX,),
            in_specs=[rows_spec, *hidden_specs],
            out_specs=units_spec,
            scratch_shapes=[pltpu.VMEM((SLOTS, 256), BF)],
        ),
        compiler_params=pltpu.CompilerParams(vmem_limit_bytes=LIMIT),
        cost_estimate=pl.CostEstimate(
            flops=2 * SLOTS * ff * width, bytes_accessed=8000000, transcendentals=0
        ),
    )(place, rows, mine, lent)
    flat = (EXPERTS * NZ * CAP, 128)
    return (w_down_grad, gate_pre_grad.reshape(flat), up_pre_grad.reshape(flat), gate_grad.T)


def solution(mesh):
    fine = Mesh(mesh.devices.reshape(EXPERTS, NZ, NX, 2), ("y", "z", "x", "c"))
    e, t = ("y", "z"), ("x", "c")
    return jax.shard_map(
        per_device,
        mesh=fine,
        in_specs=(P(e, t), P(e, None), P(e, None), P(e, t), P(None, e + t), P(None, e + t)),
        out_specs=(P(e, t), P(None, e + t), P(None, e + t), P(e, None)),
        check_vma=False,
    )
```

```python
import jax
import jax.numpy as jnp
from jax import lax
from jax.experimental import pallas as pl
from jax.experimental.pallas import tpu as pltpu
from jax.sharding import Mesh
from jax.sharding import PartitionSpec as P

EXPERTS = 8
CAP = 24
NZ = 8
NX = 4
BLOCK = EXPERTS * CAP
SLOTS = NZ * BLOCK
PART = SLOTS // 2
BF = jnp.bfloat16
F32 = jnp.float32
LIMIT = 52 * 2**20
WHOLE = pl.BlockSpec()
CHUNK = SLOTS // 4


def call(body, outs, ins, cost):
    return pl.pallas_call(
        body,
        out_shape=[jax.ShapeDtypeStruct(s, d) for s, d in outs],
        in_specs=[WHOLE] * len(ins),
        out_specs=[WHOLE] * len(outs),
        compiler_params=pltpu.CompilerParams(vmem_limit_bytes=LIMIT),
        cost_estimate=pl.CostEstimate(flops=cost[0], bytes_accessed=cost[1], transcendentals=0),
    )(*ins)


def dot(a, b, da, db):
    return lax.dot_general(a, b, (((da,), (db,)), ((), ())), preferred_element_type=F32)


def pack_body(routes, gates_ref, rows, out):
    gates = gates_ref[...].astype(F32)
    tokens = rows.shape[0]
    expert = lax.broadcasted_iota(jnp.int32, (EXPERTS, tokens), 0)
    first, second = routes[0:1, :] == expert, routes[1:2, :] == expert
    weight = jnp.where(first, gates[0:1, :], 0.0) + jnp.where(second, gates[1:2, :], 0.0)
    member = jnp.where(first | second, 1.0, 0.0)
    at = lax.broadcasted_iota(jnp.int32, (tokens, tokens), 0)
    to = lax.broadcasted_iota(jnp.int32, (tokens, tokens), 1)
    earlier = jnp.where(at < to, 1.0, 0.0).astype(BF)
    rank = dot(member.astype(BF), earlier, 1, 0)
    rank = jnp.where(member > 0.0, rank, -1.0).astype(jnp.int32)
    place = lax.broadcasted_iota(jnp.int32, (CAP, tokens), 0)
    chosen = [
        jnp.where(rank[e : e + 1] == place, weight[e : e + 1], 0.0) for e in range(EXPERTS)
    ]
    out[...] = dot(jnp.concatenate(chosen, axis=0).astype(BF), rows[...], 1, 0).astype(BF)


def act_body(gate, up, hidden):
    for z in range(NZ):
        a = gate[:, z].astype(F32).reshape(BLOCK, 128)
        b = up[:, z].astype(F32).reshape(BLOCK, 128)
        sig = 1.0 / (1.0 + jnp.exp(-a))
        hidden[z // 4, pl.ds(z % 4 * BLOCK, BLOCK), :] = (a * sig * b).astype(BF)


def x_of(label, place):
    mask = jnp.where(label == 1, 3 - 2 * place[1], jnp.where(label == 2, 1 + 2 * place[1], label - label // 3))
    return place[0] ^ mask


def swapped(label):
    return jnp.where(label == 1, 2, jnp.where(label == 2, 1, label))


def product_body(place, rows, w, mine, lent, parts, dots, total):
    label = pl.program_id(0)

    @pl.when(label == 0)
    def _():
        total[...] = jnp.zeros_like(total)

    for k in range(4):
        at = pl.ds(k * CHUNK, CHUNK)
        part = dot(rows[at, :], w[...], 1, 1)
        here = pl.ds(k % 2 * CHUNK, CHUNK)
        for i in range(2):
            unit = part[:, i * 128 : i * 128 + 128]
            parts[i, at, :] = unit.astype(BF)
            hidden = jnp.where(place[1] == k // 2, mine[0, i, here, :], lent[0, i, here, :])
            total[at, :] += unit * hidden.astype(F32)

    @pl.when(label == NX - 1)
    def _():
        dots[...] = lax.dot_general(
            jnp.ones((8, 128), F32), total[...], (((1,), (1,)), ((), ())),
            precision=lax.Precision.HIGHEST, preferred_element_type=F32,
        )


def weight_body(place, rows, mine, lent, out, units):
    for half in range(2):
        for i in range(2):
            hidden = jnp.where(place[1] == half, mine[0, i], lent[0, i])
            units[pl.ds(half * PART, PART), pl.ds(i * 128, 128)] = hidden
    out[...] = dot(units[...], rows[...], 0, 0).astype(BF)


def grad_body(hidden_grad, gate, up, gate_out, up_out):
    for z in range(NZ):
        src = hidden_grad[pl.ds(z * BLOCK, BLOCK), :].astype(F32).reshape(EXPERTS, CAP, 128)
        a, b = gate[:, z].astype(F32), up[:, z].astype(F32)
        sig = 1.0 / (1.0 + jnp.exp(-a))
        gate_out[:, z] = (src * b * sig * (1.0 + a * (1.0 - sig))).astype(BF)
        up_out[:, z] = (src * (a * sig)).astype(BF)


def per_device(grad_out, routes, gates, w_down, gate_pre, up_pre):
    xi, ci = lax.axis_index("x"), lax.axis_index("c")
    tokens, width = grad_out.shape
    ff = w_down.shape[0]
    place = jnp.stack([xi, ci]).astype(jnp.int32)

    def swap_core(x):
        return lax.ppermute(x, "c", [(0, 1), (1, 0)])

    def swap_x(x, first):
        masks = (1, 3) if first else (3, 1)
        return lax.ppermute(
            x, ("x", "c"), [(i * 2 + c, (i ^ masks[c]) * 2 + c) for i in range(NX) for c in range(2)]
        )

    routes_t, gates_t = routes.T, gates.T
    (packed,) = call(
        pack_body, [((BLOCK, width), BF)], (routes_t, gates_t, grad_out), (2 * BLOCK * tokens * width, 400000)
    )
    own = lax.all_to_all(
        packed.reshape(EXPERTS, CAP, width), "y", split_axis=0, concat_axis=0, tiled=True
    ).reshape(BLOCK, width)
    rows = lax.all_gather(own, "z", axis=0, tiled=True)

    view = (EXPERTS, NZ, CAP, 128)
    gate_late, up_late, _ = lax.optimization_barrier((gate_pre, up_pre, own))
    gate_view, up_view = gate_late.reshape(view), up_late.reshape(view)
    (hid,) = call(
        act_body, [((2, PART, 128), BF)], (gate_view, up_view), (20 * SLOTS * 128, 2000000)
    )
    keep = lax.dynamic_index_in_dim(hid, ci, 0, keepdims=False)
    got = swap_core(lax.dynamic_index_in_dim(hid, 1 - ci, 0, keepdims=False))
    h0 = jnp.stack([jnp.where(ci == 0, keep, got), jnp.where(ci == 0, got, keep)])
    h2 = swap_x(h0, True)
    h1 = swap_x(h0, False)
    h3 = swap_x(h2, False)
    mine = jnp.stack([h0, h1, h2, h3])
    lent = swap_core(mine)
    rows, lent = lax.optimization_barrier((rows, lent))

    hidden_specs = [
        pl.BlockSpec((1, 2, PART, 128), lambda i, place: (i, 0, 0, 0)),
        pl.BlockSpec((1, 2, PART, 128), lambda i, place: (swapped(i), 0, 0, 0)),
    ]
    rows_spec = pl.BlockSpec((SLOTS, width), lambda i, place: (0, 0))
    units_spec = pl.BlockSpec((ff // NX, width), lambda i, place: (x_of(i, place), 0))
    parts, dots = pl.pallas_call(
        product_body,
        out_shape=[
            jax.ShapeDtypeStruct((2 * NX, SLOTS, 128), BF),
            jax.ShapeDtypeStruct((8, SLOTS), F32),
        ],
        grid_spec=pltpu.PrefetchScalarGridSpec(
            num_scalar_prefetch=1,
            grid=(NX,),
            in_specs=[rows_spec, units_spec, *hidden_specs],
            out_specs=[
                pl.BlockSpec((2, SLOTS, 128), lambda i, place: (x_of(i, place), 0, 0)),
                pl.BlockSpec((8, SLOTS), lambda i, place: (0, 0)),
            ],
            scratch_shapes=[pltpu.VMEM((SLOTS, 128), F32)],
        ),
        compiler_params=pltpu.CompilerParams(vmem_limit_bytes=LIMIT),
        cost_estimate=pl.CostEstimate(
            flops=2 * SLOTS * ff * width, bytes_accessed=11000000, transcendentals=0
        ),
    )(place, rows, w_down, mine, lent)
    hidden_grad = lax.psum_scatter(parts, ("x", "c"), scatter_dimension=0)
    gate_pre_grad, up_pre_grad = call(
        grad_body, [(view, BF), (view, BF)], (hidden_grad, gate_view, up_view), (4 * SLOTS * 128, 3000000)
    )

    back = lax.all_to_all(
        dots[0].reshape(NZ, EXPERTS, CAP).transpose(1, 0, 2).reshape(EXPERTS * NZ, CAP),
        ("y", "z"), split_axis=0, concat_axis=0, tiled=True,
    )
    totals = jnp.sum(back.reshape(EXPERTS, NZ, CAP), axis=1)
    totals = totals + swap_core(totals)
    totals = totals + swap_x(totals, True)
    totals = totals + swap_x(totals, False)

    named = routes_t[:, None, :] == jnp.arange(EXPERTS, dtype=jnp.int32)[None, :, None]
    member = jnp.any(named, axis=0)
    order = jnp.arange(tokens, dtype=jnp.int32)
    earlier = (order[:, None] < order[None, :]).astype(BF)
    rank = jnp.dot(member.astype(BF), earlier, preferred_element_type=F32).astype(jnp.int32)
    chosen = member[:, None, :] & (rank[:, None, :] == jnp.arange(CAP, dtype=jnp.int32)[None, :, None])
    by_token = jnp.sum(jnp.where(chosen, totals[:, :, None], 0.0), axis=1)
    gate_grad = jnp.sum(jnp.where(named, by_token[None], 0.0), axis=1) / gates_t.astype(F32)

    w_down_grad = pl.pallas_call(
        weight_body,
        out_shape=jax.ShapeDtypeStruct((ff, width), BF),
        grid_spec=pltpu.PrefetchScalarGridSpec(
            num_scalar_prefetch=1,
            grid=(NX,),
            in_specs=[rows_spec, *hidden_specs],
            out_specs=units_spec,
            scratch_shapes=[pltpu.VMEM((SLOTS, 256), BF)],
        ),
        compiler_params=pltpu.CompilerParams(vmem_limit_bytes=LIMIT),
        cost_estimate=pl.CostEstimate(
            flops=2 * SLOTS * ff * width, bytes_accessed=8000000, transcendentals=0
        ),
    )(place, rows, mine, lent)
    flat = (EXPERTS * NZ * CAP, 128)
    return (w_down_grad, gate_pre_grad.reshape(flat), up_pre_grad.reshape(flat), gate_grad.T)


def solution(mesh):
    fine = Mesh(mesh.devices.reshape(EXPERTS, NZ, NX, 2), ("y", "z", "x", "c"))
    e, t = ("y", "z"), ("x", "c")
    return jax.shard_map(
        per_device,
        mesh=fine,
        in_specs=(P(e, t), P(e, None), P(e, None), P(e, t), P(None, e + t), P(None, e + t)),
        out_specs=(P(e, t), P(None, e + t), P(None, e + t), P(e, None)),
        check_vma=False,
    )
```
